256 devices in a mesh: node: 4 (over y), wide: 64 (over x, z, core).
Axes of the slice: x: 4, y: 4, z: 8, core: 2. Of those that a mesh axis runs over, the one named last changes fastest.
Arguments:
- queries: bfloat16 [65536, 1024], P(('node', 'wide')), may hold values from -300 to 300
- keys: bfloat16 [65536, 128], P(('node', 'wide')), may hold values from -7 to 7
- values: bfloat16 [65536, 128], P(('node', 'wide')), may hold values from -6 to 6
- out_grad: bfloat16 [65536, 1024], P(('node', 'wide')), may hold values from -6 to 6
- doc_lengths: int32 [128], replicated, may hold values from 1 to 2048, 65536 in all
Outputs:
- attn_out: bfloat16 [65536, 1024], P(('node', 'wide'))
- grad_queries: bfloat16 [65536, 1024], P(('node', 'wide'))
- grad_keys: bfloat16 [65536, 128], P(('node', 'wide'))
- grad_values: bfloat16 [65536, 128], P(('node', 'wide'))
The draws below stay inside these ranges and needn't reach their ends.
All inputs are finite; a program needn't handle non-finite values.
Results may differ from the reference program's by a relative error of at most 0.04.
Values may be sent and summed in bfloat16 or wider, within the bound.
No kernel may reach another device: no remote copies, remote signals or barrier semaphores. Data moves between devices by JAX's collectives and lax.ppermute only.
A program may use at most 128 MiB of HBM per device.

```python
import math
import jax
import jax.numpy as jnp
import numpy as np
from jax import lax

QHEADS = 8
HEAD_DIM = 128
WINDOW = 8
TOK_DEV = 256
TOKENS = 65536
MAXDOC = 2048
NDOCS = 128


def base_keys(key):
    return jnp.clip(jax.random.normal(key, (TOKENS, HEAD_DIM), jnp.float32), -6.0, 6.0)


def draw_keys(key, part):
    source = key
    base = base_keys(source)
    result = base
    return result.astype(jnp.bfloat16)


def draw_queries(key, part):
    key = jax.random.fold_in(key, 5)
    drawn = jnp.clip(jax.random.normal(key, (TOKENS, QHEADS * HEAD_DIM), jnp.float32), -6.0, 6.0)
    return drawn.astype(jnp.bfloat16)


def shard_levels(key, shape, split, smallest, top_value):
    factor_of, own = 1.0, jax.random.fold_in(key, 6)
    for dim, shards_of in split:
        steps = jnp.exp(jax.random.uniform(jax.random.fold_in(own, dim), (shards_of,), jnp.float32, smallest / len(split), top_value / len(split)))
        factor_of = factor_of * jnp.repeat(steps, shape[dim] // shards_of).reshape([-1 if axis == dim else 1 for axis in range(len(shape))])
    return factor_of


def length_profile(count, total, bound, lean):
    portions = [(1 << 20) // math.isqrt(rank ** lean) + 1 for rank in range(2, count + 1)]
    surplus, counts = total - bound - (count - 1), [1] * (count - 1)
    while surplus > 0:
        free = [i for i in range(count - 1) if counts[i] < bound]
        mass, left = sum([portions[i] for i in free]), surplus
        for i in free:
            addition = min(bound - counts[i], max(1, left * portions[i] // mass), surplus)
            counts[i] = counts[i] + addition
            surplus = surplus - addition
    return np.array([bound] + counts)


def ragged_sizes(key, amount, total, limit, slope):
    if amount == 2:
        one = jax.random.randint(key, (), max(1, total - limit), min(limit, total - 1) + 1)
        return jnp.stack([one, total - one])
    sizes = jnp.asarray(length_profile(amount, total, limit, slope), jnp.int32)
    couples = (amount - 1) // 2
    donor, receiver = sizes[1:1 + 2 * couples:2], sizes[2:2 + 2 * couples:2]
    margin = jnp.minimum(donor - 1, limit - receiver)
    moved = jax.random.randint(jax.random.fold_in(key, 1), (couples,), 0, 1 << 20) % (margin + 1)
    sizes = sizes.at[1:1 + 2 * couples:2].set(donor - moved).at[2:2 + 2 * couples:2].set(receiver + moved)
    return sizes[jax.random.permutation(jax.random.fold_in(key, 2), amount)]


def bell_draw(rng, dims, scale, most, shards=(), held_as=jnp.bfloat16):
    values = scale * jax.random.normal(rng, dims, jnp.float32)
    if shards:
        values = values * shard_levels(rng, dims, shards, -0.22, 0.18)
    return jnp.clip(values, -most, most).astype(held_as)


def setup_inputs(seed: int = 0) -> dict:
    key_list = jax.random.split(jax.random.key(seed), 6)
    queries = draw_queries(jax.random.fold_in(key_list[5], 71), 0)
    keys = draw_keys(jax.random.fold_in(key_list[5], 71), 0)
    values = bell_draw(key_list[2], (TOKENS, HEAD_DIM), 1.0, 6.0, ((0, 256),))
    out_grad = bell_draw(key_list[3], (TOKENS, QHEADS * HEAD_DIM), 1.0, 6.0, ((0, 256),))
    doc_lengths = ragged_sizes(key_list[4], NDOCS, TOKENS, MAXDOC, 2).astype(jnp.int32)
    return dict(queries=queries, keys=keys, values=values, out_grad=out_grad, doc_lengths=doc_lengths)


def doc_index(positions, doc_ends):
    return lax.optimization_barrier(jnp.sum((positions[:, None] >= doc_ends[None, :]).astype(jnp.int32), axis=1))

def block_masks(device, tok_rows, blocks_count, doc_ends):
    local = jnp.arange(tok_rows, dtype=jnp.int32)
    query_pos = device * tok_rows + local
    query_doc = doc_index(query_pos, doc_ends)
    offsets = jnp.arange(blocks_count, dtype=jnp.int32)
    key_pos = (device - offsets)[:, None] * tok_rows + local[None, :]
    key_doc = doc_index(key_pos.reshape(-1), doc_ends).reshape(blocks_count, tok_rows)
    same_doc = key_doc[:, None, :] == query_doc[None, :, None]
    causal = key_pos[:, None, :] <= query_pos[None, :, None]
    return same_doc & causal & (key_pos[:, None, :] >= 0)

def attention_core(queries3, grads3, blocks, masks):
    heads = queries3.shape[1]
    head_dim = queries3.shape[2]
    tok_rows = queries3.shape[0]
    score_scale = 1.0 / math.sqrt(head_dim)
    query_wide = queries3.astype(jnp.float32)
    grad_wide = grads3.astype(jnp.float32)
    high = lax.Precision.HIGHEST

    def scores_of(block):
        return jnp.einsum('thd,ud->htu', query_wide, block[:, :head_dim].astype(jnp.float32), precision=high) * score_scale

    def stat_step(carry, pair):
        block, allowed = pair

        def compute():
            running_max, running_sum = carry
            scores = jnp.where(allowed[None], scores_of(block), -1e+30)
            new_max = jnp.maximum(running_max, lax.optimization_barrier(jnp.max(scores, axis=-1)))
            terms = jnp.where(allowed[None], jnp.exp(scores - new_max[..., None]), 0.0)
            return (new_max, running_sum * jnp.exp(running_max - new_max) + lax.optimization_barrier(jnp.sum(terms, axis=-1)))
        return (lax.cond(jnp.any(allowed), compute, lambda: carry), None)
    start = (jnp.full((heads, tok_rows), -1e+30, jnp.float32), jnp.zeros((heads, tok_rows), jnp.float32))
    (row_max, row_sum), _ = lax.scan(stat_step, start, (blocks, masks))
    log_total = row_max + jnp.log(row_sum)

    def probs_of(block, allowed):
        return jnp.where(allowed[None], jnp.exp(scores_of(block) - log_total[..., None]), 0.0).astype(jnp.bfloat16)

    def out_step(total, pair):
        block, allowed = pair

        def compute():
            weights = probs_of(block, allowed).astype(jnp.float32)
            return total + jnp.einsum('htu,ud->thd', weights, block[:, head_dim:].astype(jnp.float32), precision=high)
        return (lax.cond(jnp.any(allowed), compute, lambda: total), None)
    out_sum, _ = lax.scan(out_step, jnp.zeros((tok_rows, heads, head_dim), jnp.float32), (blocks, masks))
    output = out_sum.astype(jnp.bfloat16)
    delta = lax.optimization_barrier(jnp.sum(grad_wide * output.astype(jnp.float32), axis=2)).T

    def grad_step(dq_sum, pair):
        block, allowed = pair

        def compute():
            weights = probs_of(block, allowed).astype(jnp.float32)
            key_part = block[:, :head_dim].astype(jnp.float32)
            value_part = block[:, head_dim:].astype(jnp.float32)
            dprob = jnp.einsum('thd,ud->htu', grad_wide, value_part, precision=high)
            dscore = (weights * (dprob - delta[..., None])).astype(jnp.bfloat16).astype(jnp.float32)
            new_dq = dq_sum + jnp.einsum('htu,ud->thd', dscore, key_part, precision=high)
            key_grad = jnp.einsum('htu,thd->ud', dscore, query_wide, precision=high) * score_scale
            value_grad = jnp.einsum('htu,thd->ud', weights, grad_wide, precision=high)
            return (new_dq, jnp.concatenate([key_grad, value_grad], axis=1))
        fallback = (dq_sum, jnp.zeros((tok_rows, 2 * head_dim), jnp.float32))
        return lax.cond(jnp.any(allowed), compute, lambda: fallback)
    dq_sum, partials = lax.scan(grad_step, jnp.zeros((tok_rows, heads, head_dim), jnp.float32), (blocks, masks))
    return (output, (dq_sum * score_scale).astype(jnp.bfloat16), partials)

def reference(queries, keys, values, out_grad, doc_lengths):
    doc_ends = jnp.cumsum(doc_lengths).astype(jnp.int32)
    own_all = jnp.concatenate([keys, values], axis=1)
    padded = jnp.concatenate([jnp.zeros((WINDOW * TOK_DEV, 2 * HEAD_DIM), jnp.bfloat16), own_all], axis=0)
    device_count = TOKENS // TOK_DEV

    def visit(totals, device):
        start = device * TOK_DEV
        queries3 = lax.dynamic_slice_in_dim(queries, start, TOK_DEV, 0).reshape(TOK_DEV, QHEADS, HEAD_DIM)
        grads3 = lax.dynamic_slice_in_dim(out_grad, start, TOK_DEV, 0).reshape(TOK_DEV, QHEADS, HEAD_DIM)
        blocks = jnp.stack([lax.dynamic_slice_in_dim(padded, ((device - offset + WINDOW) * TOK_DEV).astype(jnp.int32), TOK_DEV, 0) for offset in range(WINDOW + 1)])
        masks = block_masks(device, TOK_DEV, WINDOW + 1, doc_ends)
        output, grad_q, partials = attention_core(queries3, grads3, blocks, masks)
        for offset in range(WINDOW + 1):
            row = ((device - offset + WINDOW) * TOK_DEV).astype(jnp.int32)
            current = lax.dynamic_slice_in_dim(totals, row, TOK_DEV, 0)
            totals = lax.dynamic_update_slice_in_dim(totals, current + partials[offset], row, 0)
        return (totals, (output.reshape(TOK_DEV, QHEADS * HEAD_DIM), grad_q.reshape(TOK_DEV, QHEADS * HEAD_DIM)))
    start_totals = jnp.zeros(((device_count + WINDOW) * TOK_DEV, 2 * HEAD_DIM), jnp.float32)
    totals, (outputs, grads) = lax.scan(visit, start_totals, jnp.arange(device_count, dtype=jnp.int32))
    attn_out = outputs.reshape(TOKENS, QHEADS * HEAD_DIM)
    grad_queries = grads.reshape(TOKENS, QHEADS * HEAD_DIM)
    grad_keys = totals[WINDOW * TOK_DEV:, :HEAD_DIM].astype(jnp.bfloat16)
    grad_values = totals[WINDOW * TOK_DEV:, HEAD_DIM:].astype(jnp.bfloat16)
    return (attn_out, grad_queries, grad_keys, grad_values)
```

```python
import functools
import math

import jax
import jax.numpy as jnp
from jax import lax
from jax.experimental import pallas as pl
from jax.experimental.pallas import tpu as pltpu
from jax.sharding import PartitionSpec as P

AXES = ("node", "wide")
REACH = 4
GROUP = 4
MASKED = -1e30
VMEM_LIMIT = 48 * 1024 * 1024


def shifted(shard, by):
    peers = lax.axis_size(AXES)
    pairs = [(i, i + by) for i in range(peers) if 0 <= i + by < peers]
    return lax.ppermute(shard, AXES, pairs)


def swapped(shard):
    peers = lax.axis_size(AXES)
    return lax.ppermute(shard, AXES, [(i, i ^ 1) for i in range(peers)])


def dot_nt(a, b):
    return lax.dot_general(a, b, (((1,), (1,)), ((), ())), preferred_element_type=jnp.float32)


def dot_nn(a, b):
    return lax.dot_general(a, b, (((1,), (0,)), ((), ())), preferred_element_type=jnp.float32)


def stack_heads(ref, dim):
    return jnp.concatenate([ref[:, h * dim : (h + 1) * dim] for h in range(GROUP)], axis=0)


def fwd_body(rows, dim, count, diag, first, final, *refs):
    refs = list(refs)
    info, start, q = refs[:3]
    blocks = refs[3 : 3 + count]
    rest = refs[3 + count :]
    if not first:
        m_in, l_in, acc_in = rest[:3]
        rest = rest[3:]
    if final:
        grad = rest[0]
        rest = rest[1:]
    probs, m_out, m_run, l_run, acc = rest[:5]
    rest = rest[5:]
    if final:
        out, delta = rest[:2]
        rest = rest[2:]
    value_t = rest[0]
    fold = math.log2(math.e) / math.sqrt(dim)

    @pl.when(pl.program_id(0) == 0)
    def _():
        for b in range(count):
            value_t[b] = blocks[b][:, dim:].astype(jnp.float32).T.astype(jnp.bfloat16)

    queries = stack_heads(q, dim)
    if not first:
        m_run[...] = m_in[...]
        l_run[...] = l_in[...]
        acc[...] = acc_in[...]

    def work(b):
        own = diag and b == 0
        fresh = first and b == 0
        scores = dot_nt(blocks[b][:, :dim], queries)
        key_pos = lax.broadcasted_iota(jnp.int32, (rows, rows), 0) + info[2 * b]
        allowed = key_pos >= start[...]
        if own:
            allowed = allowed & (key_pos <= lax.broadcasted_iota(jnp.int32, (rows, rows), 1))
        for h in range(GROUP):
            lanes = pl.ds(h * rows, rows)
            s = jnp.where(allowed, scores[:, h * rows : (h + 1) * rows], MASKED)
            top = jnp.max(s, axis=0, keepdims=True)
            if fresh:
                m = top
            else:
                old = m_run[:, lanes]
                m = jnp.maximum(old, top)
                alpha = jnp.exp2((old - m) * fold)
            p = jnp.exp2((s - m) * fold)
            total = jnp.sum(p, axis=0, keepdims=True)
            pb = p.astype(jnp.bfloat16)
            probs[b, :, lanes] = pb
            part = dot_nn(value_t[b], pb)
            if fresh:
                l_run[:, lanes] = total
                acc[:, lanes] = part
            else:
                l_run[:, lanes] = l_run[:, lanes] * alpha + total
                acc[:, lanes] = acc[:, lanes] * alpha + part
            m_run[:, lanes] = m
            m_out[b, :, lanes] = m

    for b in range(count):
        if diag and b == 0:
            work(b)
        else:
            pl.when(info[2 * b + 1] != 0)(functools.partial(work, b))

    if final:
        for h in range(GROUP):
            lanes = pl.ds(h * rows, rows)
            cols = pl.ds(h * dim, dim)
            inverse = 1.0 / l_run[:, lanes]
            o_t = (acc[:, lanes] * inverse).astype(jnp.bfloat16).astype(jnp.float32)
            out[:, cols] = o_t.T.astype(jnp.bfloat16)
            g_t = grad[:, cols].astype(jnp.float32).T
            delta[:, lanes] = jnp.sum(o_t * g_t, axis=0, keepdims=True)
            l_run[:, lanes] = inverse


def bwd_body(rows, dim, count, first, last, *refs):
    refs = list(refs)
    info, q, grad, probs, m_then, m_fin, inverse, delta = refs[:8]
    blocks = refs[8 : 8 + count]
    rest = refs[8 + count :]
    if not first:
        dq_in = rest[0]
        rest = rest[1:]
    dq = rest[0]
    outs = rest[1 : 1 + count]
    rest = rest[1 + count :]
    key_t, dkv = rest[:2]
    dq_acc = rest[2] if last else dq
    fold = math.log2(math.e) / math.sqrt(dim)
    scale = 1.0 / math.sqrt(dim)

    @pl.when(pl.program_id(0) == 0)
    def _():
        dkv[...] = jnp.zeros_like(dkv)
        for b in range(count):
            key_t[b] = blocks[b][:, :dim].astype(jnp.float32).T.astype(jnp.bfloat16)

    queries = stack_heads(q, dim)
    grads = stack_heads(grad, dim)
    dq_acc[...] = jnp.zeros_like(dq_acc) if first else dq_in[...]

    def work(b):
        dprob = dot_nt(blocks[b][:, dim:], grads)
        ps, ds = [], []
        for h in range(GROUP):
            lanes = pl.ds(h * rows, rows)
            c = jnp.exp2((m_then[b, :, lanes] - m_fin[:, lanes]) * fold) * inverse[:, lanes]
            p = probs[b, :, lanes].astype(jnp.float32) * c
            d = (p * (dprob[:, h * rows : (h + 1) * rows] - delta[:, lanes])).astype(jnp.bfloat16)
            ps.append(p.astype(jnp.bfloat16))
            ds.append(d)
            dq_acc[:, lanes] += dot_nn(key_t[b], d)
        dkv[b, :, :dim] += dot_nn(jnp.concatenate(ds, axis=1), queries)
        dkv[b, :, dim:] += dot_nn(jnp.concatenate(ps, axis=1), grads)

    for b in range(count):
        pl.when(info[2 * b + 1] != 0)(functools.partial(work, b))

    if last:
        for h in range(GROUP):
            lanes = pl.ds(h * rows, rows)
            dq[:, h * dim : (h + 1) * dim] = (dq_acc[:, lanes] * scale).T.astype(jnp.bfloat16)

    @pl.when(pl.program_id(0) == pl.num_programs(0) - 1)
    def _():
        for b in range(count):
            outs[b][:, :dim] = (dkv[b, :, :dim] * scale).astype(outs[b].dtype)
            outs[b][:, dim:] = dkv[b, :, dim:].astype(outs[b].dtype)


def specs_of(rows, dim):
    width = GROUP * rows
    whole = lambda *shape: pl.BlockSpec(shape, lambda g: (0,) * len(shape))
    return dict(
        info=pl.BlockSpec(memory_space=pltpu.SMEM),
        start=whole(1, rows),
        heads=pl.BlockSpec((rows, GROUP * dim), lambda g: (0, g)),
        block=whole(rows, 2 * dim),
        row=pl.BlockSpec((1, width), lambda g: (0, g)),
        tall=pl.BlockSpec((dim, width), lambda g: (0, g)),
        probs=lambda n: pl.BlockSpec((n, rows, width), lambda g: (0, 0, g)),
        rows=lambda n: pl.BlockSpec((n, 1, width), lambda g: (0, 0, g)),
    )


def forward(info, start, queries, blocks, state, grad, diag):
    rows, dim = blocks[0].shape[0], blocks[0].shape[1] // 2
    heads = queries.shape[1] // dim
    count, first, final = len(blocks), state is None, grad is not None
    s = specs_of(rows, dim)
    width = heads * rows
    args = [info, start, queries, *blocks]
    in_specs = [s["info"], s["start"], s["heads"]] + [s["block"]] * count
    if not first:
        args += list(state)
        in_specs += [s["row"], s["row"], s["tall"]]
    if final:
        args.append(grad)
        in_specs.append(s["heads"])
    f32 = jnp.float32
    out_shape = [
        jax.ShapeDtypeStruct((count, rows, width), jnp.bfloat16),
        jax.ShapeDtypeStruct((count, 1, width), f32),
        jax.ShapeDtypeStruct((1, width), f32),
        jax.ShapeDtypeStruct((1, width), f32),
        jax.ShapeDtypeStruct((dim, width), f32),
    ]
    out_specs = [s["probs"](count), s["rows"](count), s["row"], s["row"], s["tall"]]
    if final:
        out_shape += [
            jax.ShapeDtypeStruct((rows, heads * dim), jnp.bfloat16),
            jax.ShapeDtypeStruct((1, width), f32),
        ]
        out_specs += [s["heads"], s["row"]]
    return pl.pallas_call(
        functools.partial(fwd_body, rows, dim, count, diag, first, final),
        grid=(heads // GROUP,),
        in_specs=in_specs,
        out_specs=out_specs,
        out_shape=out_shape,
        scratch_shapes=[pltpu.VMEM((count, dim, rows), jnp.bfloat16)],
        compiler_params=pltpu.CompilerParams(vmem_limit_bytes=VMEM_LIMIT),
        cost_estimate=pl.CostEstimate(
            flops=4 * count * rows * width * dim,
            bytes_accessed=3 * count * rows * width,
            transcendentals=count * rows * width,
        ),
    )(*args)


def backward(info, queries, grad, probs, m_then, m_fin, inverse, delta, blocks, dq, out_types, last):
    rows, dim = blocks[0].shape[0], blocks[0].shape[1] // 2
    heads = queries.shape[1] // dim
    count, first = len(blocks), dq is None
    s = specs_of(rows, dim)
    width = heads * rows
    args = [info, queries, grad, probs, m_then, m_fin, inverse, delta, *blocks]
    in_specs = [s["info"], s["heads"], s["heads"], s["probs"](count), s["rows"](count)]
    in_specs += [s["row"]] * 3 + [s["block"]] * count
    if not first:
        args.append(dq)
        in_specs.append(s["tall"])
    if last:
        out_shape = [jax.ShapeDtypeStruct((rows, heads * dim), jnp.bfloat16)]
        out_specs = [s["heads"]]
    else:
        out_shape = [jax.ShapeDtypeStruct((dim, width), jnp.float32)]
        out_specs = [s["tall"]]
    out_shape += [jax.ShapeDtypeStruct((rows, 2 * dim), t) for t in out_types]
    out_specs += [s["block"]] * count
    scratch = [
        pltpu.VMEM((count, dim, rows), jnp.bfloat16),
        pltpu.VMEM((count, rows, 2 * dim), jnp.float32),
    ]
    if last:
        scratch.append(pltpu.VMEM((dim, GROUP * rows), jnp.float32))
    return pl.pallas_call(
        functools.partial(bwd_body, rows, dim, count, first, last),
        grid=(heads // GROUP,),
        in_specs=in_specs,
        out_specs=out_specs,
        out_shape=out_shape,
        scratch_shapes=scratch,
        compiler_params=pltpu.CompilerParams(vmem_limit_bytes=VMEM_LIMIT),
        cost_estimate=pl.CostEstimate(
            flops=8 * count * rows * width * dim,
            bytes_accessed=3 * count * rows * width,
            transcendentals=0,
        ),
    )(*args)


def on_device(queries, keys, values, out_grad, doc_lengths):
    rows, dim = keys.shape
    f32, bf16 = jnp.float32, jnp.bfloat16
    device = lax.axis_index(AXES)
    odd = device % 2
    doc_ends = jnp.cumsum(doc_lengths)
    here = device * rows
    pos = here + jnp.arange(rows, dtype=jnp.int32)
    start = jnp.max(jnp.where(doc_ends[:, None] <= pos[None, :], doc_ends[:, None], 0), axis=0)
    start = (start - here)[None, :]
    first_start = start[0, 0]

    def info_of(chips):
        base = []
        for chip in chips:
            base += [jnp.int32(-2 * chip * rows), (-2 * chip + 1 - 2 * odd) * rows]
        base = jnp.stack(base)
        active = (base + rows > first_start) & (base <= 0)
        return jnp.stack([base, active.astype(jnp.int32)], axis=1).reshape(-1)

    own = jnp.concatenate([keys, values], axis=1)
    mine = [own]
    mine.append(shifted(own, 2))
    mine.append(shifted(own, 4))
    other = list(swapped(jnp.stack(mine[:3])))
    mine.append(shifted(mine[2], 2))
    mine.append(shifted(mine[2], 4))
    other += list(swapped(jnp.stack(mine[3:])))
    pair = lambda chips: [x for c in chips for x in (mine[c], other[c])]

    near, far = (0, 1, 2), (3, 4)
    info_n, info_f = info_of(near), info_of(far)
    probs_n, m_n, m1, l1, acc1 = forward(info_n, start, queries, pair(near), None, None, True)
    probs_f, m_f, m_fin, inverse, _, out, delta = forward(
        info_f, start, queries, pair(far), (m1, l1, acc1), out_grad, False
    )
    dq, m3, o3, m4, o4 = backward(
        info_f, queries, out_grad, probs_f, m_f, m_fin, inverse, delta, pair(far), None,
        (f32, bf16) * 2, False,
    )
    grad_q, m0, o0, m1_, o1, m2, o2 = backward(
        info_n, queries, out_grad, probs_n, m_n, m_fin, inverse, delta, pair(near), dq,
        (f32, bf16) * 3, True,
    )
    got = swapped(jnp.stack([o3, o4]))
    t3 = (m3 + got[0].astype(f32)).astype(bf16)
    t4 = (m4 + got[1].astype(f32)).astype(bf16)
    r4 = shifted(t4, -4)
    r3 = shifted(t3, -2)
    got = swapped(jnp.stack([o0, o1, o2]))
    t2 = (m2 + got[2].astype(f32) + r4.astype(f32) + r3.astype(f32)).astype(bf16)
    t1 = (m1_ + got[1].astype(f32)).astype(bf16)
    r2 = shifted(t2, -4)
    r1 = shifted(t1, -2)
    total = m0 + got[0].astype(f32) + r1.astype(f32) + r2.astype(f32)
    return (out, grad_q, total[:, :dim].astype(bf16), total[:, dim:].astype(bf16))


def solution(mesh):
    rows = P(AXES, None)
    return jax.shard_map(
        on_device,
        mesh=mesh,
        in_specs=(rows, rows, rows, rows, P()),
        out_specs=(rows, rows, rows, rows),
        check_vma=False,
    )
```

```python
import functools
import math

import jax
import jax.numpy as jnp
from jax import lax
from jax.experimental import pallas as pl
from jax.experimental.pallas import tpu as pltpu
from jax.sharding import PartitionSpec as P

AXES = ("node", "wide")
MASKED = -1e30
VMEM_LIMIT = 16 * 1024 * 1024
HERE = pl.BlockSpec(memory_space=pltpu.VMEM)


def shifted(shard, by):
    peers = lax.axis_size(AXES)
    pairs = [(i, i + by) for i in range(peers) if 0 <= i + by < peers]
    return lax.ppermute(shard, AXES, pairs)


def swapped(shard):
    peers = lax.axis_size(AXES)
    return lax.ppermute(shard, AXES, [(i, i ^ 1) for i in range(peers)])


def dot_nt(a, b):
    return lax.dot_general(a, b, (((1,), (1,)), ((), ())), preferred_element_type=jnp.float32)


def dot_nn(a, b):
    return lax.dot_general(a, b, (((1,), (0,)), ((), ())), preferred_element_type=jnp.float32)


def prep_body(keys, values, lengths, own, meta):
    rows, dim = keys.shape
    docs = lengths.shape[1]
    own[:, :dim] = keys[...]
    own[:, dim:] = values[...]
    device = lax.axis_index(AXES[0]) * lax.axis_size(AXES[1]) + lax.axis_index(AXES[1])
    here = device * rows
    later = lax.broadcasted_iota(jnp.int32, (docs, docs), 0)
    earlier = lax.broadcasted_iota(jnp.int32, (docs, docs), 1)
    counted = jnp.where(earlier <= later, lengths[...].astype(jnp.float32), 0.0)
    ends = jnp.sum(counted, axis=1, keepdims=True)
    pos = (lax.broadcasted_iota(jnp.int32, (docs, rows), 1) + here).astype(jnp.float32)
    start = jnp.max(jnp.where(ends <= pos, ends, 0.0), axis=0, keepdims=True)
    meta[0:1, :] = start.astype(jnp.int32) - here
    meta[1:2, :] = jnp.full((1, rows), device % 2, jnp.int32)


def prepare(keys, values, lengths):
    rows, dim = keys.shape
    return pl.pallas_call(
        prep_body,
        in_specs=[HERE] * 3,
        out_specs=[HERE] * 2,
        out_shape=[
            jax.ShapeDtypeStruct((rows, 2 * dim), keys.dtype),
            jax.ShapeDtypeStruct((2, rows), jnp.int32),
        ],
        compiler_params=pltpu.CompilerParams(vmem_limit_bytes=VMEM_LIMIT),
    )(keys, values, lengths)


def stage_body(plan, *refs):
    rows, dim, heads = plan["rows"], plan["dim"], plan["heads"]
    fwd, bwd = plan["fwd"], plan["bwd"]
    ref = dict(zip(plan["names"], refs))
    fold = math.log2(math.e) / math.sqrt(dim)
    scale = 1.0 / math.sqrt(dim)
    bf16, f32 = jnp.bfloat16, jnp.float32
    meta = ref["meta"]
    start = meta[0:1, :]
    earliest = jnp.min(start)
    odd = jnp.max(meta[1:2, :])
    blocks = sorted(set(fwd) | set(bwd))
    cols = [slice(h * dim, (h + 1) * dim) for h in range(heads)]
    lanes = [slice(h * rows, (h + 1) * rows) for h in range(heads)]

    def place(chip, side):
        return (side * (1 - 2 * odd) - 2 * chip) * rows

    def needed(chip, side):
        return (place(chip, side) + rows > earliest) & (place(chip, side) <= 0)

    if plan["first"]:
        for h in range(heads):
            g = ref["g"][:, cols[h]]
            ref["qs"][lanes[h], :] = ref["q"][:, cols[h]]
            ref["gs"][lanes[h], :] = g
            ref["gt"][:, lanes[h]] = g.T
        ref["m"][...] = jnp.full_like(ref["m"], MASKED)
        ref["l"][...] = jnp.zeros_like(ref["l"])
        ref["acc"][...] = jnp.zeros_like(ref["acc"])

    def load(chip, side):
        block, i = ref["kv", chip, side], blocks.index((chip, side))
        if (chip, side) in fwd:
            ref["vt"][i] = block[:, dim:].T
        if (chip, side) in bwd:
            ref["kt"][i] = block[:, :dim].T

    for block in blocks:
        pl.when(needed(*block))(functools.partial(load, *block))

    def fwd_block(chip, side):
        i = blocks.index((chip, side))
        key_pos = lax.broadcasted_iota(jnp.int32, (rows, rows), 0) + place(chip, side)
        allowed = (key_pos >= start) & (
            key_pos <= lax.broadcasted_iota(jnp.int32, (rows, rows), 1)
        )
        ref["bias"][...] = jnp.where(allowed, 0.0, MASKED)
        block_k, value_t = ref["kv", chip, side][:, :dim], ref["vt"][i]
        bias = jnp.concatenate([ref["bias"][...]] * 8, axis=1)
        for h in range(0, heads, 8):
            wide = slice(h * rows, (h + 8) * rows)
            s = dot_nt(block_k, ref["qs"][wide, :]) + bias
            old = ref["m"][:, wide]
            m = jnp.maximum(old, jnp.max(s, axis=0, keepdims=True))
            alpha = jnp.exp2((old - m) * fold)
            p = jnp.exp2((s - m) * fold)
            pb = p.astype(bf16)
            ref["probs", chip, side][:, wide] = pb
            total = jnp.sum(p, axis=0, keepdims=True)
            ref["l"][:, wide] = ref["l"][:, wide] * alpha + total
            ref["acc"][:, wide] = ref["acc"][:, wide] * alpha + dot_nn(value_t, pb)
            ref["m"][:, wide] = m
            ref["then", chip, side][:, wide] = m

    def finish():
        for h in range(heads):
            inverse = 1.0 / ref["l"][:, lanes[h]]
            o_t = (ref["acc"][:, lanes[h]] * inverse).astype(bf16)
            ref["out_t"][:, lanes[h]] = o_t
            terms = o_t.astype(f32) * ref["gt"][:, lanes[h]].astype(f32)
            ref["delta"][:, lanes[h]] = jnp.sum(terms, axis=0, keepdims=True)
            ref["l"][:, lanes[h]] = inverse
        ref["dq"][...] = jnp.zeros_like(ref["dq"])

    def bwd_block(chip, side):
        i = blocks.index((chip, side))
        block_v, key_t = ref["kv", chip, side][:, dim:], ref["kt"][i]
        dk = dv = None
        for h in range(0, heads, 8):
            wide = slice(h * rows, (h + 8) * rows)
            dprob = dot_nn(block_v, ref["gt"][:, wide])
            m_then = ref["then", chip, side][:, wide]
            c = jnp.exp2((m_then - ref["m"][:, wide]) * fold) * ref["l"][:, wide]
            p = ref["probs", chip, side][:, wide].astype(f32) * c
            d = (p * (dprob - ref["delta"][:, wide])).astype(bf16)
            p = p.astype(bf16)
            ref["dq"][:, wide] += dot_nn(key_t, d)
            dk_part = dot_nn(d, ref["qs"][wide, :])
            dv_part = dot_nn(p, ref["gs"][wide, :])
            dk = dk_part if dk is None else dk + dk_part
            dv = dv_part if dv is None else dv + dv_part
        part = ref["part", chip, side]
        part[:, :dim] = (dk * scale).astype(part.dtype)
        part[:, dim:] = dv.astype(part.dtype)

    for block in fwd:
        pl.when(needed(*block))(functools.partial(fwd_block, *block))
    if plan["final"]:
        finish()
    for block in bwd:
        part = ref["part", *block]
        pl.when(needed(*block))(functools.partial(bwd_block, *block))

        @pl.when(jnp.logical_not(needed(*block)))
        def _():
            part[...] = jnp.zeros_like(part)

    if plan["last"]:
        for h in range(heads):
            ref["out"][:, cols[h]] = ref["out_t"][:, lanes[h]].T
            ref["grad_q"][:, cols[h]] = (ref["dq"][:, lanes[h]] * scale).astype(bf16).T


def stage(state, fwd=(), bwd=(), final=False, last=False):
    rows, dim2 = state["kv", 0, 0].shape
    dim = dim2 // 2
    heads = state["q"].shape[1] // dim
    width = heads * rows
    bf16, f32 = jnp.bfloat16, jnp.float32
    shape = jax.ShapeDtypeStruct
    blocks = sorted(set(fwd) | set(bwd))
    first = (0, 0) in fwd
    row, tall = shape((1, width), f32), shape((dim, width), f32)
    ins, outs, both = ["meta"], {}, []
    if first:
        ins += ["q", "g"]
        outs.update(qs=shape((width, dim), bf16), gs=shape((width, dim), bf16), gt=shape((dim, width), bf16))
    else:
        ins.append("qs")
        if final or bwd:
            ins.append("gt")
        if bwd:
            ins.append("gs")
    ins += [("kv", *b) for b in blocks]
    if fwd:
        for b in fwd:
            outs["probs", *b] = shape((rows, width), bf16)
            outs["then", *b] = row
        outs.update(m=row, l=row, acc=tall)
        if not first:
            both += ["m", "l", "acc"]
    if final:
        outs.update(out_t=shape((dim, width), bf16), delta=row, dq=tall)
    if bwd:
        for b in bwd:
            if b not in fwd:
                ins += [("probs", *b), ("then", *b)]
            outs["part", *b] = shape((rows, dim2), bf16 if b[1] else f32)
        if not final:
            ins += ["m", "l", "delta"]
            outs["dq"] = tall
            both.append("dq")
    if last:
        ins.append("out_t")
        outs["out"] = outs["grad_q"] = shape((rows, heads * dim), bf16)
    out_names = list(outs)
    scratch = {}
    if fwd:
        scratch["vt"] = pltpu.VMEM((len(blocks), dim, rows), bf16)
        scratch["bias"] = pltpu.VMEM((rows, rows), f32)
    if bwd:
        scratch["kt"] = pltpu.VMEM((len(blocks), dim, rows), bf16)
    names = ins + [("in", b) for b in both] + out_names + list(scratch)
    plan = dict(
        rows=rows, dim=dim, heads=heads, fwd=fwd, bwd=bwd, first=first, final=final, last=last, names=names
    )
    products = 2 * len(fwd) + 4 * len(bwd)
    results = pl.pallas_call(
        functools.partial(stage_body, plan),
        in_specs=[HERE] * (len(ins) + len(both)),
        out_specs=[HERE] * len(out_names),
        out_shape=[outs[n] for n in out_names],
        scratch_shapes=list(scratch.values()),
        input_output_aliases={len(ins) + i: out_names.index(b) for i, b in enumerate(both)},
        compiler_params=pltpu.CompilerParams(vmem_limit_bytes=VMEM_LIMIT),
        cost_estimate=pl.CostEstimate(
            flops=2 * products * rows * width * dim, bytes_accessed=2**20, transcendentals=0
        ),
    )(*[state[n] for n in ins + both])
    state.update(zip(out_names, results))


def after(x, *others):
    return lax.optimization_barrier((x, *others))[0]


def pairs(*chips):
    return [(chip, side) for chip in chips for side in (0, 1)]


def on_device(queries, keys, values, out_grad, doc_lengths):
    rows, dim = keys.shape
    f32, bf16 = jnp.float32, jnp.bfloat16
    own, meta = prepare(keys, values, doc_lengths[None, :])
    state = {"meta": meta, "q": queries, "g": out_grad, ("kv", 0, 0): own}

    def arrive(chip, block):
        state["kv", chip, 0] = block
        state["kv", chip, 1] = swapped(block)

    back2 = shifted(own, 4)
    back1 = shifted(own, 2)
    arrive(0, own)
    stage(state, fwd=pairs(0))
    back2 = after(back2, state["l"])
    back4 = shifted(back2, 4)
    back3 = shifted(back2, 2)
    arrive(2, back2)
    arrive(1, after(back1, state["l"]))
    stage(state, fwd=pairs(1, 2))
    arrive(3, after(back3, state["l"]))
    arrive(4, after(back4, state["l"]))
    stage(state, fwd=pairs(3, 4), bwd=pairs(4), final=True)

    def summed(chip, *others):
        other = swapped(after(state["part", chip, 1], *others))
        return state["part", chip, 0] + other.astype(f32)

    t4 = summed(4).astype(bf16)
    r4 = shifted(t4, -4)
    state["dq"] = after(state["dq"], t4)
    stage(state, bwd=pairs(1, 3) + [(0, 1)])
    other = swapped(after(state["part", 0, 1], r4))
    t3 = summed(3, r4).astype(bf16)
    t1 = summed(1, r4).astype(bf16)
    r3 = shifted(t3, -2)
    r1 = shifted(t1, -2)
    state["dq"] = after(state["dq"], t1, t3)
    stage(state, bwd=pairs(2))
    t2 = (summed(2, r1, r3) + r4.astype(f32) + r3.astype(f32)).astype(bf16)
    r2 = shifted(t2, -4)
    state["dq"] = after(state["dq"], t2)
    stage(state, bwd=[(0, 0)], last=True)
    total = state["part", 0, 0] + other.astype(f32) + r1.astype(f32) + r2.astype(f32)
    return (state["out"], state["grad_q"], total[:, :dim].astype(bf16), total[:, dim:].astype(bf16))


def solution(mesh):
    rows = P(AXES, None)
    return jax.shard_map(
        on_device,
        mesh=mesh,
        in_specs=(rows, rows, rows, rows, P()),
        out_specs=(rows, rows, rows, rows),
        check_vma=False,
    )
```

```python
import functools
import math

import jax
import jax.numpy as jnp
from jax import lax
from jax.experimental import pallas as pl
from jax.experimental.pallas import tpu as pltpu
from jax.sharding import PartitionSpec as P

AXES = ("node", "wide")
MASKED = -1e30
VMEM_LIMIT = 16 * 1024 * 1024
HERE = pl.BlockSpec(memory_space=pltpu.VMEM)


def shifted(shard, by):
    peers = lax.axis_size(AXES)
    pairs = [(i, i + by) for i in range(peers) if 0 <= i + by < peers]
    return lax.ppermute(shard, AXES, pairs)


def swapped(shard):
    peers = lax.axis_size(AXES)
    return lax.ppermute(shard, AXES, [(i, i ^ 1) for i in range(peers)])


def dot_nt(a, b):
    return lax.dot_general(a, b, (((1,), (1,)), ((), ())), preferred_element_type=jnp.float32)


def dot_nn(a, b):
    return lax.dot_general(a, b, (((1,), (0,)), ((), ())), preferred_element_type=jnp.float32)


def prep_body(keys, values, lengths, own, meta, held, sems):
    rows, dim = keys.shape
    docs = lengths.shape[1]
    copies = [
        pltpu.make_async_copy(keys, own.at[:, pl.ds(0, dim)], sems.at[0]),
        pltpu.make_async_copy(values, own.at[:, pl.ds(dim, dim)], sems.at[1]),
        pltpu.make_async_copy(lengths, held, sems.at[2]),
    ]
    for copy in copies:
        copy.start()
    copies[2].wait()
    device = lax.axis_index(AXES[0]) * lax.axis_size(AXES[1]) + lax.axis_index(AXES[1])
    here = device * rows
    later = lax.broadcasted_iota(jnp.int32, (docs, docs), 0)
    earlier = lax.broadcasted_iota(jnp.int32, (docs, docs), 1)
    counted = jnp.where(earlier <= later, held[...].astype(jnp.float32), 0.0)
    ends = jnp.sum(counted, axis=1, keepdims=True)
    pos = (lax.broadcasted_iota(jnp.int32, (docs, rows), 1) + here).astype(jnp.float32)
    start = jnp.max(jnp.where(ends <= pos, ends, 0.0), axis=0, keepdims=True)
    meta[0:1, :] = start.astype(jnp.int32) - here
    meta[1:2, :] = jnp.full((1, rows), device % 2, jnp.int32)
    copies[0].wait()
    copies[1].wait()


def prepare(keys, values, lengths):
    rows, dim = keys.shape
    return pl.pallas_call(
        prep_body,
        in_specs=[pl.BlockSpec(memory_space=pltpu.HBM)] * 3,
        out_specs=[HERE] * 2,
        out_shape=[
            jax.ShapeDtypeStruct((rows, 2 * dim), keys.dtype),
            jax.ShapeDtypeStruct((2, rows), jnp.int32),
        ],
        scratch_shapes=[pltpu.VMEM(lengths.shape, lengths.dtype), pltpu.SemaphoreType.DMA((3,))],
        compiler_params=pltpu.CompilerParams(vmem_limit_bytes=VMEM_LIMIT),
    )(keys, values, lengths)


def stack_body(q, g, qs, gs, gt):
    rows, dim = q.shape[0], qs.shape[1]
    for h in range(q.shape[1] // dim):
        cols, lanes = slice(h * dim, (h + 1) * dim), slice(h * rows, (h + 1) * rows)
        qs[lanes, :] = q[:, cols]
        gs[lanes, :] = g[:, cols]
        gt[:, lanes] = g[:, cols].T


def stack(queries, grad, dim):
    rows, wide = queries.shape
    tall = jax.ShapeDtypeStruct((rows * wide // dim, dim), queries.dtype)
    return pl.pallas_call(
        stack_body,
        in_specs=[HERE] * 2,
        out_specs=[HERE] * 3,
        out_shape=[tall, tall, jax.ShapeDtypeStruct(tall.shape[::-1], queries.dtype)],
        compiler_params=pltpu.CompilerParams(vmem_limit_bytes=VMEM_LIMIT),
    )(queries, grad)


def stage_body(plan, *refs):
    rows, dim, heads = plan["rows"], plan["dim"], plan["heads"]
    fwd, bwd = plan["fwd"], plan["bwd"]
    ref = dict(zip(plan["names"], refs))
    fold = math.log2(math.e) / math.sqrt(dim)
    scale = 1.0 / math.sqrt(dim)
    bf16, f32 = jnp.bfloat16, jnp.float32
    meta = ref["meta"]
    start = meta[0:1, :]
    earliest = jnp.min(start)
    odd = jnp.max(meta[1:2, :])
    blocks = sorted(set(fwd) | set(bwd))
    cols = [slice(h * dim, (h + 1) * dim) for h in range(heads)]
    lanes = [slice(h * rows, (h + 1) * rows) for h in range(heads)]

    def place(chip, side):
        return (side * (1 - 2 * odd) - 2 * chip) * rows

    def needed(chip, side):
        return (place(chip, side) + rows > earliest) & (place(chip, side) <= 0)

    if plan["first"]:
        ref["m"][...] = jnp.full_like(ref["m"], MASKED)
        ref["l"][...] = jnp.zeros_like(ref["l"])
        ref["acc"][...] = jnp.zeros_like(ref["acc"])

    def load(chip, side):
        block, i = ref["kv", chip, side], blocks.index((chip, side))
        if (chip, side) in fwd:
            ref["vt"][i] = block[:, dim:].T
        if (chip, side) in bwd:
            ref["kt"][i] = block[:, :dim].T

    for block in blocks:
        pl.when(needed(*block))(functools.partial(load, *block))

    def fwd_block(chip, side):
        i = blocks.index((chip, side))
        key_pos = lax.broadcasted_iota(jnp.int32, (rows, rows), 0) + place(chip, side)
        allowed = (key_pos >= start) & (
            key_pos <= lax.broadcasted_iota(jnp.int32, (rows, rows), 1)
        )
        ref["bias"][...] = jnp.where(allowed, 0.0, MASKED)
        block_k, value_t = ref["kv", chip, side][:, :dim], ref["vt"][i]
        bias = jnp.concatenate([ref["bias"][...]] * 8, axis=1)
        for h in range(0, heads, 8):
            wide = slice(h * rows, (h + 8) * rows)
            s = dot_nt(block_k, ref["qs"][wide, :]) + bias
            old = ref["m"][:, wide]
            m = jnp.maximum(old, jnp.max(s, axis=0, keepdims=True))
            alpha = jnp.exp2((old - m) * fold)
            p = jnp.exp2((s - m) * fold)
            pb = p.astype(bf16)
            ref["probs", chip, side][:, wide] = pb
            total = jnp.sum(p, axis=0, keepdims=True)
            ref["l"][:, wide] = ref["l"][:, wide] * alpha + total
            ref["acc"][:, wide] = ref["acc"][:, wide] * alpha + dot_nn(value_t, pb)
            ref["m"][:, wide] = m
            ref["then", chip, side][:, wide] = m

    def finish():
        for h in range(heads):
            inverse = 1.0 / ref["l"][:, lanes[h]]
            o_t = (ref["acc"][:, lanes[h]] * inverse).astype(bf16)
            ref["out_t"][:, lanes[h]] = o_t
            terms = o_t.astype(f32) * ref["gt"][:, lanes[h]].astype(f32)
            ref["delta"][:, lanes[h]] = jnp.sum(terms, axis=0, keepdims=True)
            ref["l"][:, lanes[h]] = inverse
        ref["dq"][...] = jnp.zeros_like(ref["dq"])

    def bwd_block(chip, side):
        i = blocks.index((chip, side))
        block_v, key_t = ref["kv", chip, side][:, dim:], ref["kt"][i]
        dk = dv = None
        for h in range(0, heads, 8):
            wide = slice(h * rows, (h + 8) * rows)
            dprob = dot_nn(block_v, ref["gt"][:, wide])
            m_then = ref["then", chip, side][:, wide]
            c = jnp.exp2((m_then - ref["m"][:, wide]) * fold) * ref["l"][:, wide]
            p = ref["probs", chip, side][:, wide].astype(f32) * c
            d = (p * (dprob - ref["delta"][:, wide])).astype(bf16)
            p = p.astype(bf16)
            ref["dq"][:, wide] += dot_nn(key_t, d)
            dk_part = dot_nn(d, ref["qs"][wide, :])
            dv_part = dot_nn(p, ref["gs"][wide, :])
            dk = dk_part if dk is None else dk + dk_part
            dv = dv_part if dv is None else dv + dv_part
        part = ref["part", chip, side]
        part[:, :dim] = (dk * scale).astype(part.dtype)
        part[:, dim:] = dv.astype(part.dtype)

    for block in fwd:
        pl.when(needed(*block))(functools.partial(fwd_block, *block))
    if plan["final"]:
        finish()
    for block in bwd:
        part = ref["part", *block]
        pl.when(needed(*block))(functools.partial(bwd_block, *block))

        @pl.when(jnp.logical_not(needed(*block)))
        def _():
            part[...] = jnp.zeros_like(part)

    if plan["last"]:
        for h in range(heads):
            ref["out"][:, cols[h]] = ref["out_t"][:, lanes[h]].T
            ref["grad_q"][:, cols[h]] = (ref["dq"][:, lanes[h]] * scale).astype(bf16).T


def stage(state, fwd=(), bwd=(), final=False, last=False):
    rows, dim2 = state["kv", 0, 0].shape
    dim = dim2 // 2
    width = state["qs"].shape[0]
    heads = width // rows
    bf16, f32 = jnp.bfloat16, jnp.float32
    shape = jax.ShapeDtypeStruct
    blocks = sorted(set(fwd) | set(bwd))
    first = (0, 0) in fwd
    row, tall = shape((1, width), f32), shape((dim, width), f32)
    ins, outs, both = ["meta", "qs"], {}, []
    if final or bwd:
        ins.append("gt")
    if bwd:
        ins.append("gs")
    ins += [("kv", *b) for b in blocks]
    if fwd:
        for b in fwd:
            outs["probs", *b] = shape((rows, width), bf16)
            outs["then", *b] = row
        outs.update(m=row, l=row, acc=tall)
        if not first:
            both += ["m", "l", "acc"]
    if final:
        outs.update(out_t=shape((dim, width), bf16), delta=row, dq=tall)
    if bwd:
        for b in bwd:
            if b not in fwd:
                ins += [("probs", *b), ("then", *b)]
            outs["part", *b] = shape((rows, dim2), bf16 if b[1] else f32)
        if not final:
            ins += ["m", "l", "delta"]
            outs["dq"] = tall
            both.append("dq")
    if last:
        ins.append("out_t")
        outs["out"] = outs["grad_q"] = shape((rows, heads * dim), bf16)
    out_names = list(outs)
    scratch = {}
    if fwd:
        scratch["vt"] = pltpu.VMEM((len(blocks), dim, rows), bf16)
        scratch["bias"] = pltpu.VMEM((rows, rows), f32)
    if bwd:
        scratch["kt"] = pltpu.VMEM((len(blocks), dim, rows), bf16)
    names = ins + [("in", b) for b in both] + out_names + list(scratch)
    plan = dict(
        rows=rows, dim=dim, heads=heads, fwd=fwd, bwd=bwd, first=first, final=final, last=last, names=names
    )
    products = 2 * len(fwd) + 4 * len(bwd)
    results = pl.pallas_call(
        functools.partial(stage_body, plan),
        in_specs=[HERE] * (len(ins) + len(both)),
        out_specs=[HERE] * len(out_names),
        out_shape=[outs[n] for n in out_names],
        scratch_shapes=list(scratch.values()),
        input_output_aliases={len(ins) + i: out_names.index(b) for i, b in enumerate(both)},
        compiler_params=pltpu.CompilerParams(vmem_limit_bytes=VMEM_LIMIT),
        cost_estimate=pl.CostEstimate(
            flops=2 * products * rows * width * dim, bytes_accessed=2**20, transcendentals=0
        ),
    )(*[state[n] for n in ins + both])
    state.update(zip(out_names, results))


def after(x, *others):
    return lax.optimization_barrier((x, *others))[0]


def pairs(*chips):
    return [(chip, side) for chip in chips for side in (0, 1)]


def on_device(queries, keys, values, out_grad, doc_lengths):
    rows, dim = keys.shape
    f32, bf16 = jnp.float32, jnp.bfloat16
    own, meta = prepare(keys, values, doc_lengths[None, :])
    state = {"meta": meta, ("kv", 0, 0): own}
    state.update(zip(("qs", "gs", "gt"), stack(queries, out_grad, dim)))

    def arrive(chip, block):
        state["kv", chip, 0] = block
        state["kv", chip, 1] = swapped(block)

    back2 = shifted(own, 4)
    back1 = shifted(own, 2)
    back2 = after(back2, state["qs"])
    back4 = shifted(back2, 4)
    back3 = shifted(back2, 2)
    arrive(0, own)
    arrive(2, back2)
    arrive(1, back1)
    stage(state, fwd=pairs(0, 1, 2))
    arrive(3, after(back3, state["l"]))
    arrive(4, after(back4, state["l"]))
    stage(state, fwd=pairs(3, 4), bwd=pairs(4), final=True)

    def summed(chip, *others):
        other = swapped(after(state["part", chip, 1], *others))
        return state["part", chip, 0] + other.astype(f32)

    t4 = summed(4).astype(bf16)
    r4 = shifted(t4, -4)
    state["dq"] = after(state["dq"], t4)
    stage(state, bwd=pairs(1, 3) + [(0, 1)])
    t3 = summed(3, r4).astype(bf16)
    r3 = shifted(t3, -2)
    state["dq"] = after(state["dq"], t3)
    stage(state, bwd=pairs(2))
    t2 = (summed(2, r3) + r4.astype(f32) + r3.astype(f32)).astype(bf16)
    r2 = shifted(t2, -4)
    t1 = summed(1, state["part", 2, 0]).astype(bf16)
    r1 = shifted(after(t1, t2), -2)
    other = swapped(after(state["part", 0, 1], state["part", 2, 0]))
    state["dq"] = after(state["dq"], t1, t2)
    stage(state, bwd=[(0, 0)], last=True)
    total = state["part", 0, 0] + other.astype(f32) + r1.astype(f32) + r2.astype(f32)
    return (state["out"], state["grad_q"], total[:, :dim].astype(bf16), total[:, dim:].astype(bf16))


def solution(mesh):
    rows = P(AXES, None)
    return jax.shard_map(
        on_device,
        mesh=mesh,
        in_specs=(rows, rows, rows, rows, P()),
        out_specs=(rows, rows, rows, rows),
        check_vma=False,
    )
```

```python
import functools
import math

import jax
import jax.numpy as jnp
from jax import lax
from jax.experimental import pallas as pl
from jax.experimental.pallas import tpu as pltpu
from jax.sharding import PartitionSpec as P

AXES = ("node", "wide")
REACH = 4
MASKED = -1e30
VMEM_LIMIT = 16 * 1024 * 1024
QUICK = pl.CostEstimate(flops=1, bytes_accessed=1, transcendentals=0)
HERE = pl.BlockSpec(memory_space=pltpu.VMEM)


def shifted(shard, by):
    peers = lax.axis_size(AXES)
    pairs = [(i, i + by) for i in range(peers) if 0 <= i + by < peers]
    return lax.ppermute(shard, AXES, pairs)


def swapped(shard):
    peers = lax.axis_size(AXES)
    return lax.ppermute(shard, AXES, [(i, i ^ 1) for i in range(peers)])


def dot_nt(a, b):
    return lax.dot_general(a, b, (((1,), (1,)), ((), ())), preferred_element_type=jnp.float32)


def dot_nn(a, b):
    return lax.dot_general(a, b, (((1,), (0,)), ((), ())), preferred_element_type=jnp.float32)


def prep_body(keys, values, lengths, own, meta, held, sems):
    rows, dim = keys.shape
    docs = lengths.shape[1]
    copies = [
        pltpu.make_async_copy(keys, own.at[:, pl.ds(0, dim)], sems.at[0]),
        pltpu.make_async_copy(values, own.at[:, pl.ds(dim, dim)], sems.at[1]),
        pltpu.make_async_copy(lengths, held, sems.at[2]),
    ]
    for copy in copies:
        copy.start()
    copies[2].wait()
    device = lax.axis_index(AXES[0]) * lax.axis_size(AXES[1]) + lax.axis_index(AXES[1])
    here = device * rows
    later = lax.broadcasted_iota(jnp.int32, (docs, docs), 0)
    earlier = lax.broadcasted_iota(jnp.int32, (docs, docs), 1)
    counted = jnp.where(earlier <= later, held[...].astype(jnp.float32), 0.0)
    ends = jnp.sum(counted, axis=1, keepdims=True)
    pos = (lax.broadcasted_iota(jnp.int32, (docs, rows), 1) + here).astype(jnp.float32)
    start = jnp.max(jnp.where(ends <= pos, ends, 0.0), axis=0, keepdims=True)
    meta[0:1, :] = start.astype(jnp.int32) - here
    meta[1:2, :] = jnp.full((1, rows), device % 2, jnp.int32)
    copies[0].wait()
    copies[1].wait()


def prepare(keys, values, lengths):
    rows, dim = keys.shape
    return pl.pallas_call(
        prep_body,
        in_specs=[pl.BlockSpec(memory_space=pltpu.HBM)] * 3,
        out_specs=[HERE] * 2,
        out_shape=[
            jax.ShapeDtypeStruct((rows, 2 * dim), keys.dtype),
            jax.ShapeDtypeStruct((2, rows), jnp.int32),
        ],
        scratch_shapes=[pltpu.VMEM(lengths.shape, lengths.dtype), pltpu.SemaphoreType.DMA((3,))],
        compiler_params=pltpu.CompilerParams(vmem_limit_bytes=VMEM_LIMIT),
    )(keys, values, lengths)


def stack_body(q, g, qs, gs, gt):
    rows, dim = q.shape[0], qs.shape[1]
    for h in range(q.shape[1] // dim):
        cols, lanes = slice(h * dim, (h + 1) * dim), slice(h * rows, (h + 1) * rows)
        qs[lanes, :] = q[:, cols]
        gs[lanes, :] = g[:, cols]
        gt[:, lanes] = g[:, cols].T


def stack(queries, grad, dim):
    rows, wide = queries.shape
    tall = jax.ShapeDtypeStruct((rows * wide // dim, dim), queries.dtype)
    return pl.pallas_call(
        stack_body,
        in_specs=[HERE] * 2,
        out_specs=[HERE] * 3,
        out_shape=[tall, tall, jax.ShapeDtypeStruct(tall.shape[::-1], queries.dtype)],
        compiler_params=pltpu.CompilerParams(vmem_limit_bytes=VMEM_LIMIT),
    )(queries, grad)


def stage_body(plan, *refs):
    rows, dim, heads = plan["rows"], plan["dim"], plan["heads"]
    fwd, bwd = plan["fwd"], plan["bwd"]
    ref = dict(zip(plan["names"], refs))
    fold = math.log2(math.e) / math.sqrt(dim)
    scale = 1.0 / math.sqrt(dim)
    bf16, f32 = jnp.bfloat16, jnp.float32
    meta = ref["meta"]
    start = meta[0:1, :]
    earliest = jnp.min(start)
    odd = jnp.max(meta[1:2, :])
    blocks = sorted(set(fwd) | set(bwd))
    cols = [slice(h * dim, (h + 1) * dim) for h in range(heads)]
    lanes = [slice(h * rows, (h + 1) * rows) for h in range(heads)]

    def place(chip, side):
        return (side * (1 - 2 * odd) - 2 * chip) * rows

    def needed(chip, side):
        return (place(chip, side) + rows > earliest) & (place(chip, side) <= 0)

    if plan["first"]:
        ref["m"][...] = jnp.full_like(ref["m"], MASKED)
        ref["l"][...] = jnp.zeros_like(ref["l"])
        ref["acc"][...] = jnp.zeros_like(ref["acc"])

    def load(chip, side):
        block, i = ref["kv", chip, side], blocks.index((chip, side))
        if (chip, side) in fwd:
            ref["vt"][i] = block[:, dim:].T
        if (chip, side) in bwd:
            ref["kt"][i] = block[:, :dim].T

    for block in blocks:
        pl.when(needed(*block))(functools.partial(load, *block))

    def fwd_block(chip, side):
        i = blocks.index((chip, side))
        key_pos = lax.broadcasted_iota(jnp.int32, (rows, rows), 0) + place(chip, side)
        allowed = (key_pos >= start) & (
            key_pos <= lax.broadcasted_iota(jnp.int32, (rows, rows), 1)
        )
        ref["bias"][...] = jnp.where(allowed, 0.0, MASKED)
        block_k, value_t = ref["kv", chip, side][:, :dim], ref["vt"][i]
        bias = jnp.concatenate([ref["bias"][...]] * 8, axis=1)
        for h in range(0, heads, 8):
            wide = slice(h * rows, (h + 8) * rows)
            s = dot_nt(block_k, ref["qs"][wide, :]) + bias
            old = ref["m"][:, wide]
            m = jnp.maximum(old, jnp.max(s, axis=0, keepdims=True))
            alpha = jnp.exp2((old - m) * fold)
            p = jnp.exp2((s - m) * fold)
            pb = p.astype(bf16)
            ref["probs", chip, side][:, wide] = pb
            total = jnp.sum(p, axis=0, keepdims=True)
            ref["l"][:, wide] = ref["l"][:, wide] * alpha + total
            ref["acc"][:, wide] = ref["acc"][:, wide] * alpha + dot_nn(value_t, pb)
            ref["m"][:, wide] = m
            ref["then", chip, side][:, wide] = m

    def finish():
        for h in range(heads):
            inverse = 1.0 / ref["l"][:, lanes[h]]
            o_t = (ref["acc"][:, lanes[h]] * inverse).astype(bf16)
            ref["out_t"][:, lanes[h]] = o_t
            terms = o_t.astype(f32) * ref["gt"][:, lanes[h]].astype(f32)
            ref["delta"][:, lanes[h]] = jnp.sum(terms, axis=0, keepdims=True)
            ref["l"][:, lanes[h]] = inverse
        ref["dq"][...] = jnp.zeros_like(ref["dq"])

    def bwd_block(chip, side):
        i = blocks.index((chip, side))
        block_v, key_t = ref["kv", chip, side][:, dim:], ref["kt"][i]
        dk = dv = None
        for h in range(0, heads, 8):
            wide = slice(h * rows, (h + 8) * rows)
            dprob = dot_nn(block_v, ref["gt"][:, wide])
            m_then = ref["then", chip, side][:, wide]
            c = jnp.exp2((m_then - ref["m"][:, wide]) * fold) * ref["l"][:, wide]
            p = ref["probs", chip, side][:, wide].astype(f32) * c
            d = (p * (dprob - ref["delta"][:, wide])).astype(bf16)
            p = p.astype(bf16)
            ref["dq"][:, wide] += dot_nn(key_t, d)
            dk_part = dot_nn(d, ref["qs"][wide, :])
            dv_part = dot_nn(p, ref["gs"][wide, :])
            dk = dk_part if dk is None else dk + dk_part
            dv = dv_part if dv is None else dv + dv_part
        part = ref["part", chip, side]
        part[:, :dim] = (dk * scale).astype(part.dtype)
        part[:, dim:] = dv.astype(part.dtype)

    for block in fwd:
        pl.when(needed(*block))(functools.partial(fwd_block, *block))
    if plan["final"]:
        finish()
    for block in bwd:
        part = ref["part", *block]
        pl.when(needed(*block))(functools.partial(bwd_block, *block))

        @pl.when(jnp.logical_not(needed(*block)))
        def _():
            part[...] = jnp.zeros_like(part)

    if plan["last"]:
        for h in range(heads):
            ref["out"][:, cols[h]] = ref["out_t"][:, lanes[h]].T
            ref["grad_q"][:, cols[h]] = (ref["dq"][:, lanes[h]] * scale).astype(bf16).T


def stage(state, fwd=(), bwd=(), final=False, last=False):
    rows, dim2 = state["kv", 0, 0].shape
    dim = dim2 // 2
    width = state["qs"].shape[0]
    heads = width // rows
    bf16, f32 = jnp.bfloat16, jnp.float32
    shape = jax.ShapeDtypeStruct
    blocks = sorted(set(fwd) | set(bwd))
    first = (0, 0) in fwd
    row, tall = shape((1, width), f32), shape((dim, width), f32)
    ins, outs, both = ["meta", "qs"], {}, []
    if final or bwd:
        ins.append("gt")
    if bwd:
        ins.append("gs")
    ins += [("kv", *b) for b in blocks]
    if fwd:
        for b in fwd:
            outs["probs", *b] = shape((rows, width), bf16)
            outs["then", *b] = row
        outs.update(m=row, l=row, acc=tall)
        if not first:
            both += ["m", "l", "acc"]
    if final:
        outs.update(out_t=shape((dim, width), bf16), delta=row, dq=tall)
    if bwd:
        for b in bwd:
            if b not in fwd:
                ins += [("probs", *b), ("then", *b)]
            outs["part", *b] = shape((rows, dim2), bf16 if b[1] else f32)
        if not final:
            ins += ["m", "l", "delta"]
            outs["dq"] = tall
            both.append("dq")
    if last:
        ins.append("out_t")
        outs["out"] = outs["grad_q"] = shape((rows, heads * dim), bf16)
    out_names = list(outs)
    scratch = {}
    if fwd:
        scratch["vt"] = pltpu.VMEM((len(blocks), dim, rows), bf16)
        scratch["bias"] = pltpu.VMEM((rows, rows), f32)
    if bwd:
        scratch["kt"] = pltpu.VMEM((len(blocks), dim, rows), bf16)
    names = ins + [("in", b) for b in both] + out_names + list(scratch)
    plan = dict(
        rows=rows, dim=dim, heads=heads, fwd=fwd, bwd=bwd, first=first, final=final, last=last, names=names
    )
    results = pl.pallas_call(
        functools.partial(stage_body, plan),
        in_specs=[HERE] * (len(ins) + len(both)),
        out_specs=[HERE] * len(out_names),
        out_shape=[outs[n] for n in out_names],
        scratch_shapes=list(scratch.values()),
        input_output_aliases={len(ins) + i: out_names.index(b) for i, b in enumerate(both)},
        compiler_params=pltpu.CompilerParams(vmem_limit_bytes=VMEM_LIMIT),
        cost_estimate=QUICK,
    )(*[state[n] for n in ins + both])
    state.update(zip(out_names, results))


def after(x, *others):
    return lax.optimization_barrier((x, *others))[0]


def pairs(*chips):
    return [(chip, side) for chip in chips for side in (0, 1)]


def on_device(queries, keys, values, out_grad, doc_lengths):
    rows, dim = keys.shape
    f32, bf16 = jnp.float32, jnp.bfloat16
    own, meta = prepare(keys, values, doc_lengths[None, :])
    state = {"meta": meta, ("kv", 0, 0): own}
    state.update(zip(("qs", "gs", "gt"), stack(queries, out_grad, dim)))

    block = own
    for chip in range(REACH):
        coming = shifted(block, 2)
        state["kv", chip, 0], state["kv", chip, 1] = block, swapped(block)
        stage(state, fwd=pairs(chip))
        block = after(coming, state["l"])
    state["kv", REACH, 0], state["kv", REACH, 1] = block, swapped(block)
    stage(state, fwd=pairs(REACH), bwd=[(REACH, 0), (REACH, 1), (REACH - 1, 1)], final=True)

    passed = None
    for chip in range(REACH, -1, -1):
        total = state["part", chip, 0] + swapped(state["part", chip, 1]).astype(f32)
        if passed is not None:
            total = total + passed.astype(f32)
        if chip:
            total = total.astype(bf16)
            passed = shifted(total, -2)
            state["dq"] = after(state["dq"], total)
            todo = [(chip - 1, 0)] + [(chip - 2, 1)] * (chip > 1)
            stage(state, bwd=todo, last=chip == 1)
    return (state["out"], state["grad_q"], total[:, :dim].astype(bf16), total[:, dim:].astype(bf16))


def solution(mesh):
    rows = P(AXES, None)
    return jax.shard_map(
        on_device,
        mesh=mesh,
        in_specs=(rows, rows, rows, rows, P()),
        out_specs=(rows, rows, rows, rows),
        check_vma=False,
    )
```

```python
import functools
import math

import jax
import jax.numpy as jnp
from jax import lax
from jax.experimental import pallas as pl
from jax.experimental.pallas import tpu as pltpu
from jax.sharding import PartitionSpec as P

AXES = ("node", "wide")
MASKED = -1e30
VMEM_LIMIT = 16 * 1024 * 1024
QUICK = pl.CostEstimate(flops=1, bytes_accessed=1, transcendentals=0)
HERE = pl.BlockSpec(memory_space=pltpu.VMEM)


def shifted(shard, by):
    peers = lax.axis_size(AXES)
    pairs = [(i, i + by) for i in range(peers) if 0 <= i + by < peers]
    return lax.ppermute(shard, AXES, pairs)


def swapped(shard):
    peers = lax.axis_size(AXES)
    return lax.ppermute(shard, AXES, [(i, i ^ 1) for i in range(peers)])


def dot_nt(a, b):
    return lax.dot_general(a, b, (((1,), (1,)), ((), ())), preferred_element_type=jnp.float32)


def dot_nn(a, b):
    return lax.dot_general(a, b, (((1,), (0,)), ((), ())), preferred_element_type=jnp.float32)


def prep_body(keys, values, lengths, own, meta, held, sems):
    rows, dim = keys.shape
    docs = lengths.shape[1]
    copies = [
        pltpu.make_async_copy(keys, own.at[:, pl.ds(0, dim)], sems.at[0]),
        pltpu.make_async_copy(values, own.at[:, pl.ds(dim, dim)], sems.at[1]),
        pltpu.make_async_copy(lengths, held, sems.at[2]),
    ]
    for copy in copies:
        copy.start()
    copies[2].wait()
    device = lax.axis_index(AXES[0]) * lax.axis_size(AXES[1]) + lax.axis_index(AXES[1])
    here = device * rows
    later = lax.broadcasted_iota(jnp.int32, (docs, docs), 0)
    earlier = lax.broadcasted_iota(jnp.int32, (docs, docs), 1)
    counted = jnp.where(earlier <= later, held[...].astype(jnp.float32), 0.0)
    ends = jnp.sum(counted, axis=1, keepdims=True)
    pos = (lax.broadcasted_iota(jnp.int32, (docs, rows), 1) + here).astype(jnp.float32)
    start = jnp.max(jnp.where(ends <= pos, ends, 0.0), axis=0, keepdims=True)
    meta[0:1, :] = start.astype(jnp.int32) - here
    meta[1:2, :] = jnp.full((1, rows), device % 2, jnp.int32)
    copies[0].wait()
    copies[1].wait()


def prepare(keys, values, lengths):
    rows, dim = keys.shape
    return pl.pallas_call(
        prep_body,
        in_specs=[pl.BlockSpec(memory_space=pltpu.HBM)] * 3,
        out_specs=[HERE] * 2,
        out_shape=[
            jax.ShapeDtypeStruct((rows, 2 * dim), keys.dtype),
            jax.ShapeDtypeStruct((2, rows), jnp.int32),
        ],
        scratch_shapes=[pltpu.VMEM(lengths.shape, lengths.dtype), pltpu.SemaphoreType.DMA((3,))],
        compiler_params=pltpu.CompilerParams(vmem_limit_bytes=VMEM_LIMIT),
    )(keys, values, lengths)


def stack_body(q, g, qs, gs, gt):
    rows, dim = q.shape[0], qs.shape[1]
    for h in range(q.shape[1] // dim):
        cols, lanes = slice(h * dim, (h + 1) * dim), slice(h * rows, (h + 1) * rows)
        qs[lanes, :] = q[:, cols]
        gs[lanes, :] = g[:, cols]
        gt[:, lanes] = g[:, cols].T


def stack(queries, grad, dim):
    rows, wide = queries.shape
    tall = jax.ShapeDtypeStruct((rows * wide // dim, dim), queries.dtype)
    return pl.pallas_call(
        stack_body,
        in_specs=[HERE] * 2,
        out_specs=[HERE] * 3,
        out_shape=[tall, tall, jax.ShapeDtypeStruct(tall.shape[::-1], queries.dtype)],
        compiler_params=pltpu.CompilerParams(vmem_limit_bytes=VMEM_LIMIT),
    )(queries, grad)


def stage_body(plan, *refs):
    rows, dim, heads = plan["rows"], plan["dim"], plan["heads"]
    fwd, bwd = plan["fwd"], plan["bwd"]
    ref = dict(zip(plan["names"], refs))
    fold = math.log2(math.e) / math.sqrt(dim)
    scale = 1.0 / math.sqrt(dim)
    bf16, f32 = jnp.bfloat16, jnp.float32
    meta = ref["meta"]
    start = meta[0:1, :]
    earliest = jnp.min(start)
    odd = jnp.max(meta[1:2, :])
    blocks = sorted(set(fwd) | set(bwd))
    cols = [slice(h * dim, (h + 1) * dim) for h in range(heads)]
    lanes = [slice(h * rows, (h + 1) * rows) for h in range(heads)]

    def place(chip, side):
        return (side * (1 - 2 * odd) - 2 * chip) * rows

    def needed(chip, side):
        return (place(chip, side) + rows > earliest) & (place(chip, side) <= 0)

    if plan["first"]:
        ref["m"][...] = jnp.full_like(ref["m"], MASKED)
        ref["l"][...] = jnp.zeros_like(ref["l"])
        ref["acc"][...] = jnp.zeros_like(ref["acc"])

    def load(chip, side):
        block, i = ref["kv", chip, side], blocks.index((chip, side))
        if (chip, side) in fwd:
            ref["vt"][i] = block[:, dim:].T
        if (chip, side) in bwd:
            ref["kt"][i] = block[:, :dim].T

    for block in blocks:
        pl.when(needed(*block))(functools.partial(load, *block))

    def fwd_block(chip, side):
        i = blocks.index((chip, side))
        key_pos = lax.broadcasted_iota(jnp.int32, (rows, rows), 0) + place(chip, side)
        allowed = (key_pos >= start) & (
            key_pos <= lax.broadcasted_iota(jnp.int32, (rows, rows), 1)
        )
        ref["bias"][...] = jnp.where(allowed, 0.0, MASKED)
        block_k, value_t = ref["kv", chip, side][:, :dim], ref["vt"][i]
        bias = jnp.concatenate([ref["bias"][...]] * 8, axis=1)
        for h in range(0, heads, 8):
            wide = slice(h * rows, (h + 8) * rows)
            s = dot_nt(block_k, ref["qs"][wide, :]) + bias
            old = ref["m"][:, wide]
            m = jnp.maximum(old, jnp.max(s, axis=0, keepdims=True))
            alpha = jnp.exp2((old - m) * fold)
            p = jnp.exp2((s - m) * fold)
            pb = p.astype(bf16)
            ref["probs", chip, side][:, wide] = pb
            total = jnp.sum(p, axis=0, keepdims=True)
            ref["l"][:, wide] = ref["l"][:, wide] * alpha + total
            ref["acc"][:, wide] = ref["acc"][:, wide] * alpha + dot_nn(value_t, pb)
            ref["m"][:, wide] = m
            ref["then", chip, side][:, wide] = m

    def finish():
        for h in range(heads):
            inverse = 1.0 / ref["l"][:, lanes[h]]
            o_t = (ref["acc"][:, lanes[h]] * inverse).astype(bf16)
            ref["out_t"][:, lanes[h]] = o_t
            terms = o_t.astype(f32) * ref["gt"][:, lanes[h]].astype(f32)
            ref["delta"][:, lanes[h]] = jnp.sum(terms, axis=0, keepdims=True)
            ref["l"][:, lanes[h]] = inverse
        ref["dq"][...] = jnp.zeros_like(ref["dq"])

    def bwd_block(chip, side):
        i = blocks.index((chip, side))
        block_v, key_t = ref["kv", chip, side][:, dim:], ref["kt"][i]
        dk = dv = None
        for h in range(0, heads, 8):
            wide = slice(h * rows, (h + 8) * rows)
            dprob = dot_nn(block_v, ref["gt"][:, wide])
            m_then = ref["then", chip, side][:, wide]
            c = jnp.exp2((m_then - ref["m"][:, wide]) * fold) * ref["l"][:, wide]
            p = ref["probs", chip, side][:, wide].astype(f32) * c
            d = (p * (dprob - ref["delta"][:, wide])).astype(bf16)
            p = p.astype(bf16)
            ref["dq"][:, wide] += dot_nn(key_t, d)
            dk_part = dot_nn(d, ref["qs"][wide, :])
            dv_part = dot_nn(p, ref["gs"][wide, :])
            dk = dk_part if dk is None else dk + dk_part
            dv = dv_part if dv is None else dv + dv_part
        part = ref["part", chip, side]
        part[:, :dim] = (dk * scale).astype(part.dtype)
        part[:, dim:] = dv.astype(part.dtype)

    for block in fwd:
        pl.when(needed(*block))(functools.partial(fwd_block, *block))
    if plan["final"]:
        finish()
    for block in bwd:
        part = ref["part", *block]
        pl.when(needed(*block))(functools.partial(bwd_block, *block))

        @pl.when(jnp.logical_not(needed(*block)))
        def _():
            part[...] = jnp.zeros_like(part)

    if plan["last"]:
        for h in range(heads):
            ref["out"][:, cols[h]] = ref["out_t"][:, lanes[h]].T
            ref["grad_q"][:, cols[h]] = (ref["dq"][:, lanes[h]] * scale).astype(bf16).T


def stage(state, fwd=(), bwd=(), final=False, last=False):
    rows, dim2 = state["kv", 0, 0].shape
    dim = dim2 // 2
    width = state["qs"].shape[0]
    heads = width // rows
    bf16, f32 = jnp.bfloat16, jnp.float32
    shape = jax.ShapeDtypeStruct
    blocks = sorted(set(fwd) | set(bwd))
    first = (0, 0) in fwd
    row, tall = shape((1, width), f32), shape((dim, width), f32)
    ins, outs, both = ["meta", "qs"], {}, []
    if final or bwd:
        ins.append("gt")
    if bwd:
        ins.append("gs")
    ins += [("kv", *b) for b in blocks]
    if fwd:
        for b in fwd:
            outs["probs", *b] = shape((rows, width), bf16)
            outs["then", *b] = row
        outs.update(m=row, l=row, acc=tall)
        if not first:
            both += ["m", "l", "acc"]
    if final:
        outs.update(out_t=shape((dim, width), bf16), delta=row, dq=tall)
    if bwd:
        for b in bwd:
            if b not in fwd:
                ins += [("probs", *b), ("then", *b)]
            outs["part", *b] = shape((rows, dim2), bf16 if b[1] else f32)
        if not final:
            ins += ["m", "l", "delta"]
            outs["dq"] = tall
            both.append("dq")
    if last:
        ins.append("out_t")
        outs["out"] = outs["grad_q"] = shape((rows, heads * dim), bf16)
    out_names = list(outs)
    scratch = {}
    if fwd:
        scratch["vt"] = pltpu.VMEM((len(blocks), dim, rows), bf16)
        scratch["bias"] = pltpu.VMEM((rows, rows), f32)
    if bwd:
        scratch["kt"] = pltpu.VMEM((len(blocks), dim, rows), bf16)
    names = ins + [("in", b) for b in both] + out_names + list(scratch)
    plan = dict(
        rows=rows, dim=dim, heads=heads, fwd=fwd, bwd=bwd, first=first, final=final, last=last, names=names
    )
    results = pl.pallas_call(
        functools.partial(stage_body, plan),
        in_specs=[HERE] * (len(ins) + len(both)),
        out_specs=[HERE] * len(out_names),
        out_shape=[outs[n] for n in out_names],
        scratch_shapes=list(scratch.values()),
        input_output_aliases={len(ins) + i: out_names.index(b) for i, b in enumerate(both)},
        compiler_params=pltpu.CompilerParams(vmem_limit_bytes=VMEM_LIMIT),
        cost_estimate=QUICK,
    )(*[state[n] for n in ins + both])
    state.update(zip(out_names, results))


def after(x, *others):
    return lax.optimization_barrier((x, *others))[0]


def pairs(*chips):
    return [(chip, side) for chip in chips for side in (0, 1)]


def on_device(queries, keys, values, out_grad, doc_lengths):
    rows, dim = keys.shape
    f32, bf16 = jnp.float32, jnp.bfloat16
    own, meta = prepare(keys, values, doc_lengths[None, :])
    state = {"meta": meta, ("kv", 0, 0): own}
    state.update(zip(("qs", "gs", "gt"), stack(queries, out_grad, dim)))

    back2 = shifted(own, 4)
    back1 = shifted(own, 2)
    back2 = after(back2, state["qs"])
    back4 = shifted(back2, 4)
    back3 = shifted(back2, 2)
    state["kv", 0, 0], state["kv", 0, 1] = own, swapped(own)
    state["kv", 1, 0] = back1
    state["kv", 2, 0], state["kv", 2, 1] = back2, swapped(back2)
    stage(state, fwd=pairs(0, 2) + [(1, 0)])
    state["kv", 1, 1] = swapped(after(back1, state["l"]))
    for chip, block in ((3, back3), (4, back4)):
        block = after(block, state["l"])
        state["kv", chip, 0], state["kv", chip, 1] = block, swapped(block)
    stage(state, fwd=[(1, 1)] + pairs(3, 4), bwd=pairs(3, 4), final=True)

    def summed(chip, *others):
        other = swapped(after(state["part", chip, 1], *others))
        return state["part", chip, 0] + other.astype(f32)

    t4, t3 = summed(4).astype(bf16), summed(3).astype(bf16)
    r4, r3 = shifted(t4, -4), shifted(t3, -2)
    state["dq"] = after(state["dq"], t3, t4)
    stage(state, bwd=pairs(1, 2) + [(0, 1)])
    t2 = (summed(2, r3, r4) + r4.astype(f32) + r3.astype(f32)).astype(bf16)
    t1 = summed(1, r3, r4).astype(bf16)
    r2, r1 = shifted(t2, -4), shifted(t1, -2)
    other = swapped(after(state["part", 0, 1], r3, r4))
    state["dq"] = after(state["dq"], t1, t2)
    stage(state, bwd=[(0, 0)], last=True)
    total = state["part", 0, 0] + other.astype(f32) + r1.astype(f32) + r2.astype(f32)
    return (state["out"], state["grad_q"], total[:, :dim].astype(bf16), total[:, dim:].astype(bf16))


def solution(mesh):
    rows = P(AXES, None)
    return jax.shard_map(
        on_device,
        mesh=mesh,
        in_specs=(rows, rows, rows, rows, P()),
        out_specs=(rows, rows, rows, rows),
        check_vma=False,
    )
```

```python
import functools
import math

import jax
import jax.numpy as jnp
from jax import lax
from jax.experimental import pallas as pl
from jax.experimental.pallas import tpu as pltpu
from jax.sharding import PartitionSpec as P

AXES = ("node", "wide")
MASKED = -1e30
VMEM_LIMIT = 16 * 1024 * 1024
QUICK = pl.CostEstimate(flops=1, bytes_accessed=1, transcendentals=0)
HERE = pl.BlockSpec(memory_space=pltpu.VMEM)


def shifted(shard, by):
    peers = lax.axis_size(AXES)
    pairs = [(i, i + by) for i in range(peers) if 0 <= i + by < peers]
    return lax.ppermute(shard, AXES, pairs)


def swapped(shard):
    peers = lax.axis_size(AXES)
    return lax.ppermute(shard, AXES, [(i, i ^ 1) for i in range(peers)])


def dot_nt(a, b):
    return lax.dot_general(a, b, (((1,), (1,)), ((), ())), preferred_element_type=jnp.float32)


def dot_nn(a, b):
    return lax.dot_general(a, b, (((1,), (0,)), ((), ())), preferred_element_type=jnp.float32)


def beside(keys, values):
    dim = keys.shape[1]
    lane = lax.broadcasted_iota(jnp.int32, (keys.shape[0], 2 * dim), 1)
    none = jnp.zeros((), keys.dtype)
    left = lax.pad(keys, none, ((0, 0, 0), (0, dim, 0)))
    right = lax.pad(values, none, ((0, 0, 0), (dim, 0, 0)))
    return jnp.where(lane < dim, left, right)


def stack_body(q, g, lengths, qs, gs, gt, meta):
    rows, dim = q.shape[0], qs.shape[1]
    docs = lengths.shape[1]
    for h in range(q.shape[1] // dim):
        cols, lanes = slice(h * dim, (h + 1) * dim), slice(h * rows, (h + 1) * rows)
        qs[lanes, :] = q[:, cols]
        gs[lanes, :] = g[:, cols]
        gt[:, lanes] = g[:, cols].T
    device = lax.axis_index(AXES[0]) * lax.axis_size(AXES[1]) + lax.axis_index(AXES[1])
    here = device * rows
    later = lax.broadcasted_iota(jnp.int32, (docs, docs), 0)
    earlier = lax.broadcasted_iota(jnp.int32, (docs, docs), 1)
    counted = jnp.where(earlier <= later, lengths[...].astype(jnp.float32), 0.0)
    ends = jnp.sum(counted, axis=1, keepdims=True)
    pos = (lax.broadcasted_iota(jnp.int32, (docs, rows), 1) + here).astype(jnp.float32)
    start = jnp.max(jnp.where(ends <= pos, ends, 0.0), axis=0, keepdims=True)
    meta[0:1, :] = start.astype(jnp.int32) - here
    meta[1:2, :] = jnp.full((1, rows), device % 2, jnp.int32)


def stack(queries, grad, lengths, dim):
    rows, wide = queries.shape
    tall = jax.ShapeDtypeStruct((rows * wide // dim, dim), queries.dtype)
    return pl.pallas_call(
        stack_body,
        in_specs=[HERE] * 3,
        out_specs=[HERE] * 4,
        out_shape=[
            tall,
            tall,
            jax.ShapeDtypeStruct(tall.shape[::-1], queries.dtype),
            jax.ShapeDtypeStruct((2, rows), jnp.int32),
        ],
        compiler_params=pltpu.CompilerParams(vmem_limit_bytes=VMEM_LIMIT),
    )(queries, grad, lengths)


def stage_body(plan, *refs):
    rows, dim, heads = plan["rows"], plan["dim"], plan["heads"]
    fwd, bwd = plan["fwd"], plan["bwd"]
    ref = dict(zip(plan["names"], refs))
    fold = math.log2(math.e) / math.sqrt(dim)
    scale = 1.0 / math.sqrt(dim)
    bf16, f32 = jnp.bfloat16, jnp.float32
    meta = ref["meta"]
    start = meta[0:1, :]
    earliest, latest = jnp.min(start), jnp.max(start)
    odd = jnp.max(meta[1:2, :])
    blocks = sorted(set(fwd) | set(bwd))
    cols = [slice(h * dim, (h + 1) * dim) for h in range(heads)]
    lanes = [slice(h * rows, (h + 1) * rows) for h in range(heads)]

    def place(chip, side):
        return (side * (1 - 2 * odd) - 2 * chip) * rows

    def needed(chip, side):
        return (place(chip, side) + rows > earliest) & (place(chip, side) <= 0)

    if plan["first"]:
        ref["m"][...] = jnp.full_like(ref["m"], MASKED)
        ref["l"][...] = jnp.zeros_like(ref["l"])
        ref["acc"][...] = jnp.zeros_like(ref["acc"])

    def load(chip, side):
        block, i = ref["kv", chip, side], blocks.index((chip, side))
        if (chip, side) in fwd:
            ref["vt"][i] = block[:, dim:].T
        if (chip, side) in bwd:
            ref["kt"][i] = block[:, :dim].T

    for block in blocks:
        pl.when(needed(*block))(functools.partial(load, *block))

    def fwd_block(chip, side, masked):
        i = blocks.index((chip, side))
        if masked:
            key_pos = lax.broadcasted_iota(jnp.int32, (rows, rows), 0) + place(chip, side)
            allowed = (key_pos >= start) & (
                key_pos <= lax.broadcasted_iota(jnp.int32, (rows, rows), 1)
            )
            ref["bias"][...] = jnp.where(allowed, 0.0, MASKED)
        block_k, value_t = ref["kv", chip, side][:, :dim], ref["vt"][i]
        for h in range(0, heads, 8):
            wide = slice(h * rows, (h + 8) * rows)
            s = dot_nt(block_k, ref["qs"][wide, :])
            if masked:
                s = s + jnp.concatenate([ref["bias"][...]] * 8, axis=1)
            old = ref["m"][:, wide]
            m = jnp.maximum(old, jnp.max(s, axis=0, keepdims=True))
            alpha = jnp.exp2((old - m) * fold)
            p = jnp.exp2((s - m) * fold)
            pb = p.astype(bf16)
            ref["probs", chip, side][:, wide] = pb
            total = jnp.sum(p, axis=0, keepdims=True)
            ref["l"][:, wide] = ref["l"][:, wide] * alpha + total
            ref["acc"][:, wide] = ref["acc"][:, wide] * alpha + dot_nn(value_t, pb)
            ref["m"][:, wide] = m
            ref["then", chip, side][:, wide] = m

    def finish():
        for h in range(heads):
            inverse = 1.0 / ref["l"][:, lanes[h]]
            o_t = (ref["acc"][:, lanes[h]] * inverse).astype(bf16)
            ref["out_t"][:, lanes[h]] = o_t
            terms = o_t.astype(f32) * ref["gt"][:, lanes[h]].astype(f32)
            ref["delta"][:, lanes[h]] = jnp.sum(terms, axis=0, keepdims=True)
            ref["l"][:, lanes[h]] = inverse
        ref["dq"][...] = jnp.zeros_like(ref["dq"])

    def bwd_block(chip, side):
        i = blocks.index((chip, side))
        block_v, key_t = ref["kv", chip, side][:, dim:], ref["kt"][i]
        dk = dv = None
        for h in range(0, heads, 8):
            wide = slice(h * rows, (h + 8) * rows)
            dprob = dot_nn(block_v, ref["gt"][:, wide])
            m_then = ref["then", chip, side][:, wide]
            c = jnp.exp2((m_then - ref["m"][:, wide]) * fold) * ref["l"][:, wide]
            p = ref["probs", chip, side][:, wide].astype(f32) * c
            d = (p * (dprob - ref["delta"][:, wide])).astype(bf16)
            p = p.astype(bf16)
            ref["dq"][:, wide] += dot_nn(key_t, d)
            dk_part = dot_nn(d, ref["qs"][wide, :])
            dv_part = dot_nn(p, ref["gs"][wide, :])
            dk = dk_part if dk is None else dk + dk_part
            dv = dv_part if dv is None else dv + dv_part
        part = ref["part", chip, side]
        part[:, :dim] = (dk * scale).astype(part.dtype)
        part[:, dim:] = dv.astype(part.dtype)

    for block in fwd:
        if block == (0, 0):
            fwd_block(*block, True)
            continue
        whole = (place(*block) >= latest) & (place(*block) < 0)
        pl.when(needed(*block) & whole)(functools.partial(fwd_block, *block, False))
        pl.when(needed(*block) & jnp.logical_not(whole))(functools.partial(fwd_block, *block, True))
    if plan["final"]:
        finish()
    for block in bwd:
        part = ref["part", *block]
        pl.when(needed(*block))(functools.partial(bwd_block, *block))

        @pl.when(jnp.logical_not(needed(*block)))
        def _():
            part[...] = jnp.zeros_like(part)

    if plan["last"]:
        for h in range(heads):
            ref["out"][:, cols[h]] = ref["out_t"][:, lanes[h]].T
            ref["grad_q"][:, cols[h]] = (ref["dq"][:, lanes[h]] * scale).astype(bf16).T


def stage(state, fwd=(), bwd=(), final=False, last=False):
    rows, dim2 = state["kv", 0, 0].shape
    dim = dim2 // 2
    width = state["qs"].shape[0]
    heads = width // rows
    bf16, f32 = jnp.bfloat16, jnp.float32
    shape = jax.ShapeDtypeStruct
    blocks = sorted(set(fwd) | set(bwd))
    first = (0, 0) in fwd
    row, tall = shape((1, width), f32), shape((dim, width), f32)
    ins, outs, both = ["meta", "qs"], {}, []
    if final or bwd:
        ins.append("gt")
    if bwd:
        ins.append("gs")
    ins += [("kv", *b) for b in blocks]
    if fwd:
        for b in fwd:
            outs["probs", *b] = shape((rows, width), bf16)
            outs["then", *b] = row
        outs.update(m=row, l=row, acc=tall)
        if not first:
            both += ["m", "l", "acc"]
    if final:
        outs.update(out_t=shape((dim, width), bf16), delta=row, dq=tall)
    if bwd:
        for b in bwd:
            if b not in fwd:
                ins += [("probs", *b), ("then", *b)]
            outs["part", *b] = shape((rows, dim2), bf16 if b[1] else f32)
        if not final:
            ins += ["m", "l", "delta"]
            outs["dq"] = tall
            both.append("dq")
    if last:
        ins.append("out_t")
        outs["out"] = outs["grad_q"] = shape((rows, heads * dim), bf16)
    out_names = list(outs)
    scratch = {}
    if fwd:
        scratch["vt"] = pltpu.VMEM((len(blocks), dim, rows), bf16)
        scratch["bias"] = pltpu.VMEM((rows, rows), f32)
    if bwd:
        scratch["kt"] = pltpu.VMEM((len(blocks), dim, rows), bf16)
    names = ins + [("in", b) for b in both] + out_names + list(scratch)
    plan = dict(
        rows=rows, dim=dim, heads=heads, fwd=fwd, bwd=bwd, first=first, final=final, last=last, names=names
    )
    results = pl.pallas_call(
        functools.partial(stage_body, plan),
        in_specs=[HERE] * (len(ins) + len(both)),
        out_specs=[HERE] * len(out_names),
        out_shape=[outs[n] for n in out_names],
        scratch_shapes=list(scratch.values()),
        input_output_aliases={len(ins) + i: out_names.index(b) for i, b in enumerate(both)},
        compiler_params=pltpu.CompilerParams(vmem_limit_bytes=VMEM_LIMIT),
        cost_estimate=QUICK,
    )(*[state[n] for n in ins + both])
    state.update(zip(out_names, results))


def after(x, *others):
    return lax.optimization_barrier((x, *others))[0]


def pairs(*chips):
    return [(chip, side) for chip in chips for side in (0, 1)]


def on_device(queries, keys, values, out_grad, doc_lengths):
    rows, dim = keys.shape
    f32, bf16 = jnp.float32, jnp.bfloat16
    own = beside(keys, values)
    state = dict(zip(("qs", "gs", "gt", "meta"), stack(queries, out_grad, doc_lengths[None, :], dim)))

    back2 = shifted(own, 4)
    back1 = shifted(own, 2)
    back2 = after(back2, state["qs"])
    back4 = shifted(back2, 4)
    back3 = shifted(back2, 2)
    state["kv", 0, 0], state["kv", 0, 1] = own, swapped(own)
    state["kv", 1, 0] = back1
    state["kv", 2, 0], state["kv", 2, 1] = back2, swapped(back2)
    stage(state, fwd=pairs(0, 2) + [(1, 0)])
    state["kv", 1, 1] = swapped(after(back1, state["l"]))
    for chip, block in ((3, back3), (4, back4)):
        block = after(block, state["l"])
        state["kv", chip, 0], state["kv", chip, 1] = block, swapped(block)
    stage(state, fwd=[(1, 1)] + pairs(3, 4), bwd=pairs(3, 4), final=True)

    def summed(chip, *others):
        other = swapped(after(state["part", chip, 1], *others))
        return state["part", chip, 0] + other.astype(f32)

    t4, t3 = summed(4).astype(bf16), summed(3).astype(bf16)
    r4, r3 = shifted(t4, -4), shifted(t3, -2)
    state["dq"] = after(state["dq"], t3, t4)
    stage(state, bwd=pairs(1, 2) + [(0, 1)])
    t2 = (summed(2, r3, r4) + r4.astype(f32) + r3.astype(f32)).astype(bf16)
    t1 = summed(1, r3, r4).astype(bf16)
    r2, r1 = shifted(t2, -4), shifted(t1, -2)
    other = swapped(after(state["part", 0, 1], r3, r4))
    state["dq"] = after(state["dq"], t1, t2)
    stage(state, bwd=[(0, 0)], last=True)
    total = state["part", 0, 0] + other.astype(f32) + r1.astype(f32) + r2.astype(f32)
    return (state["out"], state["grad_q"], total[:, :dim].astype(bf16), total[:, dim:].astype(bf16))


def solution(mesh):
    rows = P(AXES, None)
    return jax.shard_map(
        on_device,
        mesh=mesh,
        in_specs=(rows, rows, rows, rows, P()),
        out_specs=(rows, rows, rows, rows),
        check_vma=False,
    )
```

```python
import functools
import math

import jax
import jax.numpy as jnp
from jax import lax
from jax.experimental import pallas as pl
from jax.experimental.pallas import tpu as pltpu
from jax.sharding import PartitionSpec as P

AXES = ("node", "wide")
MASKED = -1e30
VMEM_LIMIT = 16 * 1024 * 1024
QUICK = pl.CostEstimate(flops=1, bytes_accessed=1, transcendentals=0)
HERE = pl.BlockSpec(memory_space=pltpu.VMEM)


def shifted(shard, by):
    peers = lax.axis_size(AXES)
    pairs = [(i, i + by) for i in range(peers) if 0 <= i + by < peers]
    return lax.ppermute(shard, AXES, pairs)


def swapped(shard):
    peers = lax.axis_size(AXES)
    return lax.ppermute(shard, AXES, [(i, i ^ 1) for i in range(peers)])


def dot_nt(a, b):
    return lax.dot_general(a, b, (((1,), (1,)), ((), ())), preferred_element_type=jnp.float32)


def dot_nn(a, b):
    return lax.dot_general(a, b, (((1,), (0,)), ((), ())), preferred_element_type=jnp.float32)


def beside(keys, values):
    dim = keys.shape[1]
    lane = lax.broadcasted_iota(jnp.int32, (keys.shape[0], 2 * dim), 1)
    none = jnp.zeros((), keys.dtype)
    left = lax.pad(keys, none, ((0, 0, 0), (0, dim, 0)))
    right = lax.pad(values, none, ((0, 0, 0), (dim, 0, 0)))
    return jnp.where(lane < dim, left, right)


def stack_body(q, g, lengths, qs, gs, gt, meta):
    rows, dim = q.shape[0], qs.shape[1]
    docs = lengths.shape[1]
    for h in range(q.shape[1] // dim):
        cols, lanes = slice(h * dim, (h + 1) * dim), slice(h * rows, (h + 1) * rows)
        qs[lanes, :] = q[:, cols]
        gs[lanes, :] = g[:, cols]
        gt[:, lanes] = g[:, cols].T
    device = lax.axis_index(AXES[0]) * lax.axis_size(AXES[1]) + lax.axis_index(AXES[1])
    here = device * rows
    later = lax.broadcasted_iota(jnp.int32, (docs, docs), 0)
    earlier = lax.broadcasted_iota(jnp.int32, (docs, docs), 1)
    counted = jnp.where(earlier <= later, lengths[...].astype(jnp.float32), 0.0)
    ends = jnp.sum(counted, axis=1, keepdims=True)
    pos = (lax.broadcasted_iota(jnp.int32, (docs, rows), 1) + here).astype(jnp.float32)
    start = jnp.max(jnp.where(ends <= pos, ends, 0.0), axis=0, keepdims=True)
    meta[0:1, :] = start.astype(jnp.int32) - here
    meta[1:2, :] = jnp.full((1, rows), device % 2, jnp.int32)


def stack(queries, grad, lengths, dim):
    rows, wide = queries.shape
    tall = jax.ShapeDtypeStruct((rows * wide // dim, dim), queries.dtype)
    return pl.pallas_call(
        stack_body,
        in_specs=[HERE] * 3,
        out_specs=[HERE] * 4,
        out_shape=[
            tall,
            tall,
            jax.ShapeDtypeStruct(tall.shape[::-1], queries.dtype),
            jax.ShapeDtypeStruct((2, rows), jnp.int32),
        ],
        compiler_params=pltpu.CompilerParams(vmem_limit_bytes=VMEM_LIMIT),
    )(queries, grad, lengths)


def stage_body(plan, *refs):
    rows, dim, heads = plan["rows"], plan["dim"], plan["heads"]
    fwd, bwd = plan["fwd"], plan["bwd"]
    ref = dict(zip(plan["names"], refs))
    fold = math.log2(math.e) / math.sqrt(dim)
    scale = 1.0 / math.sqrt(dim)
    bf16, f32 = jnp.bfloat16, jnp.float32
    meta = ref["meta"]
    start = meta[0:1, :]
    earliest = jnp.min(start)
    odd = jnp.max(meta[1:2, :])
    blocks = sorted(set(fwd) | set(bwd))
    cols = [slice(h * dim, (h + 1) * dim) for h in range(heads)]
    lanes = [slice(h * rows, (h + 1) * rows) for h in range(heads)]

    def place(chip, side):
        return (side * (1 - 2 * odd) - 2 * chip) * rows

    def needed(chip, side):
        return (place(chip, side) + rows > earliest) & (place(chip, side) <= 0)

    if plan["first"]:
        ref["m"][...] = jnp.full_like(ref["m"], MASKED)
        ref["l"][...] = jnp.zeros_like(ref["l"])
        ref["acc"][...] = jnp.zeros_like(ref["acc"])

    def load(chip, side):
        block, i = ref["kv", chip, side], blocks.index((chip, side))
        if (chip, side) in fwd:
            ref["vt"][i] = block[:, dim:].T
        if (chip, side) in bwd:
            ref["kt"][i] = block[:, :dim].T

    for block in blocks:
        pl.when(needed(*block))(functools.partial(load, *block))

    def fwd_block(chip, side):
        i = blocks.index((chip, side))
        key_pos = lax.broadcasted_iota(jnp.int32, (rows, rows), 0) + place(chip, side)
        allowed = (key_pos >= start) & (
            key_pos <= lax.broadcasted_iota(jnp.int32, (rows, rows), 1)
        )
        ref["bias"][...] = jnp.where(allowed, 0.0, MASKED)
        block_k, value_t = ref["kv", chip, side][:, :dim], ref["vt"][i]
        for h in range(0, heads, 8):
            wide = slice(h * rows, (h + 8) * rows)
            s = dot_nt(block_k, ref["qs"][wide, :]) + jnp.concatenate([ref["bias"][...]] * 8, axis=1)
            old = ref["m"][:, wide]
            m = jnp.maximum(old, jnp.max(s, axis=0, keepdims=True))
            alpha = jnp.exp2((old - m) * fold)
            p = jnp.exp2((s - m) * fold)
            pb = p.astype(bf16)
            ref["probs", chip, side][:, wide] = pb
            total = jnp.sum(p, axis=0, keepdims=True)
            ref["l"][:, wide] = ref["l"][:, wide] * alpha + total
            ref["acc"][:, wide] = ref["acc"][:, wide] * alpha + dot_nn(value_t, pb)
            ref["m"][:, wide] = m
            ref["then", chip, side][:, wide] = m

    def finish():
        for h in range(heads):
            inverse = 1.0 / ref["l"][:, lanes[h]]
            o_t = (ref["acc"][:, lanes[h]] * inverse).astype(bf16)
            ref["out_t"][:, lanes[h]] = o_t
            terms = o_t.astype(f32) * ref["gt"][:, lanes[h]].astype(f32)
            ref["delta"][:, lanes[h]] = jnp.sum(terms, axis=0, keepdims=True)
            ref["l"][:, lanes[h]] = inverse
        ref["dq"][...] = jnp.zeros_like(ref["dq"])

    def bwd_block(chip, side):
        i = blocks.index((chip, side))
        block_v, key_t = ref["kv", chip, side][:, dim:], ref["kt"][i]
        dk = dv = None
        for h in range(0, heads, 8):
            wide = slice(h * rows, (h + 8) * rows)
            dprob = dot_nn(block_v, ref["gt"][:, wide])
            m_then = ref["then", chip, side][:, wide]
            c = jnp.exp2((m_then - ref["m"][:, wide]) * fold) * ref["l"][:, wide]
            p = ref["probs", chip, side][:, wide].astype(f32) * c
            d = (p * (dprob - ref["delta"][:, wide])).astype(bf16)
            p = p.astype(bf16)
            ref["dq"][:, wide] += dot_nn(key_t, d)
            dk_part = dot_nn(d, ref["qs"][wide, :])
            dv_part = dot_nn(p, ref["gs"][wide, :])
            dk = dk_part if dk is None else dk + dk_part
            dv = dv_part if dv is None else dv + dv_part
        part = ref["part", chip, side]
        part[:, :dim] = (dk * scale).astype(part.dtype)
        part[:, dim:] = dv.astype(part.dtype)

    for block in fwd:
        pl.when(needed(*block))(functools.partial(fwd_block, *block))
    if plan["final"]:
        finish()
    for block in bwd:
        part = ref["part", *block]
        pl.when(needed(*block))(functools.partial(bwd_block, *block))

        @pl.when(jnp.logical_not(needed(*block)))
        def _():
            part[...] = jnp.zeros_like(part)

    if plan["last"]:
        for h in range(heads):
            ref["out"][:, cols[h]] = ref["out_t"][:, lanes[h]].T
            ref["grad_q"][:, cols[h]] = (ref["dq"][:, lanes[h]] * scale).astype(bf16).T


def stage(state, fwd=(), bwd=(), final=False, last=False):
    rows, dim2 = state["kv", 0, 0].shape
    dim = dim2 // 2
    width = state["qs"].shape[0]
    heads = width // rows
    bf16, f32 = jnp.bfloat16, jnp.float32
    shape = jax.ShapeDtypeStruct
    blocks = sorted(set(fwd) | set(bwd))
    first = (0, 0) in fwd
    row, tall = shape((1, width), f32), shape((dim, width), f32)
    ins, outs, both = ["meta", "qs"], {}, []
    if final or bwd:
        ins.append("gt")
    if bwd:
        ins.append("gs")
    ins += [("kv", *b) for b in blocks]
    if fwd:
        for b in fwd:
            outs["probs", *b] = shape((rows, width), bf16)
            outs["then", *b] = row
        outs.update(m=row, l=row, acc=tall)
        if not first:
            both += ["m", "l", "acc"]
    if final:
        outs.update(out_t=shape((dim, width), bf16), delta=row, dq=tall)
    if bwd:
        for b in bwd:
            if b not in fwd:
                ins += [("probs", *b), ("then", *b)]
            outs["part", *b] = shape((rows, dim2), bf16 if b[1] else f32)
        if not final:
            ins += ["m", "l", "delta"]
            outs["dq"] = tall
            both.append("dq")
    if last:
        ins.append("out_t")
        outs["out"] = outs["grad_q"] = shape((rows, heads * dim), bf16)
    out_names = list(outs)
    scratch = {}
    if fwd:
        scratch["vt"] = pltpu.VMEM((len(blocks), dim, rows), bf16)
        scratch["bias"] = pltpu.VMEM((rows, rows), f32)
    if bwd:
        scratch["kt"] = pltpu.VMEM((len(blocks), dim, rows), bf16)
    names = ins + [("in", b) for b in both] + out_names + list(scratch)
    plan = dict(
        rows=rows, dim=dim, heads=heads, fwd=fwd, bwd=bwd, first=first, final=final, last=last, names=names
    )
    results = pl.pallas_call(
        functools.partial(stage_body, plan),
        in_specs=[HERE] * (len(ins) + len(both)),
        out_specs=[HERE] * len(out_names),
        out_shape=[outs[n] for n in out_names],
        scratch_shapes=list(scratch.values()),
        input_output_aliases={len(ins) + i: out_names.index(b) for i, b in enumerate(both)},
        compiler_params=pltpu.CompilerParams(vmem_limit_bytes=VMEM_LIMIT),
        cost_estimate=QUICK,
    )(*[state[n] for n in ins + both])
    state.update(zip(out_names, results))


def after(x, *others):
    return lax.optimization_barrier((x, *others))[0]


def pairs(*chips):
    return [(chip, side) for chip in chips for side in (0, 1)]


def on_device(queries, keys, values, out_grad, doc_lengths):
    rows, dim = keys.shape
    f32, bf16 = jnp.float32, jnp.bfloat16
    own = beside(keys, values)
    state = dict(zip(("qs", "gs", "gt", "meta"), stack(queries, out_grad, doc_lengths[None, :], dim)))

    back2 = shifted(own, 4)
    back1 = shifted(own, 2)
    back2 = after(back2, state["qs"])
    back4 = shifted(back2, 4)
    back3 = shifted(back2, 2)
    state["kv", 0, 0], state["kv", 0, 1] = own, swapped(own)
    state["kv", 1, 0] = back1
    state["kv", 2, 0], state["kv", 2, 1] = back2, swapped(back2)
    stage(state, fwd=pairs(0, 2) + [(1, 0)])
    state["kv", 1, 1] = swapped(after(back1, state["l"]))
    for chip, block in ((3, back3), (4, back4)):
        block = after(block, state["l"])
        state["kv", chip, 0], state["kv", chip, 1] = block, swapped(block)
    stage(state, fwd=[(3, 0), (4, 0)])
    stage(state, fwd=[(1, 1), (3, 1), (4, 1)], bwd=[(3, 1), (4, 1)], final=True)
    stage(state, bwd=[(3, 0), (4, 0)])

    def summed(chip, *others):
        other = swapped(after(state["part", chip, 1], *others))
        return state["part", chip, 0] + other.astype(f32)

    t4, t3 = summed(4).astype(bf16), summed(3).astype(bf16)
    r4, r3 = shifted(t4, -4), shifted(t3, -2)
    state["dq"] = after(state["dq"], t3, t4)
    stage(state, bwd=pairs(1, 2) + [(0, 1)])
    t2 = (summed(2, r3, r4) + r4.astype(f32) + r3.astype(f32)).astype(bf16)
    t1 = summed(1, r3, r4).astype(bf16)
    r2, r1 = shifted(t2, -4), shifted(t1, -2)
    other = swapped(after(state["part", 0, 1], r3, r4))
    state["dq"] = after(state["dq"], t1, t2)
    stage(state, bwd=[(0, 0)], last=True)
    total = state["part", 0, 0] + other.astype(f32) + r1.astype(f32) + r2.astype(f32)
    return (state["out"], state["grad_q"], total[:, :dim].astype(bf16), total[:, dim:].astype(bf16))


def solution(mesh):
    rows = P(AXES, None)
    return jax.shard_map(
        on_device,
        mesh=mesh,
        in_specs=(rows, rows, rows, rows, P()),
        out_specs=(rows, rows, rows, rows),
        check_vma=False,
    )
```

```python
import functools
import math

import jax
import jax.numpy as jnp
from jax import lax
from jax.experimental import pallas as pl
from jax.experimental.pallas import tpu as pltpu
from jax.sharding import PartitionSpec as P

AXES = ("node", "wide")
MASKED = -1e30
VMEM_LIMIT = 16 * 1024 * 1024
QUICK = pl.CostEstimate(flops=1, bytes_accessed=1, transcendentals=0)
HERE = pl.BlockSpec(memory_space=pltpu.VMEM)


def shifted(shard, by):
    peers = lax.axis_size(AXES)
    pairs = [(i, i + by) for i in range(peers) if 0 <= i + by < peers]
    return lax.ppermute(shard, AXES, pairs)


def swapped(shard):
    peers = lax.axis_size(AXES)
    return lax.ppermute(shard, AXES, [(i, i ^ 1) for i in range(peers)])


def dot_nt(a, b):
    return lax.dot_general(a, b, (((1,), (1,)), ((), ())), preferred_element_type=jnp.float32)


def dot_nn(a, b):
    return lax.dot_general(a, b, (((1,), (0,)), ((), ())), preferred_element_type=jnp.float32)


def beside(keys, values):
    dim = keys.shape[1]
    lane = lax.broadcasted_iota(jnp.int32, (keys.shape[0], 2 * dim), 1)
    none = jnp.zeros((), keys.dtype)
    left = lax.pad(keys, none, ((0, 0, 0), (0, dim, 0)))
    right = lax.pad(values, none, ((0, 0, 0), (dim, 0, 0)))
    return jnp.where(lane < dim, left, right)


def stack_body(q, g, lengths, qs, gs, gt, meta):
    rows, dim = q.shape[0], qs.shape[1]
    docs = lengths.shape[1]
    for h in range(q.shape[1] // dim):
        cols, lanes = slice(h * dim, (h + 1) * dim), slice(h * rows, (h + 1) * rows)
        qs[lanes, :] = q[:, cols]
        gs[lanes, :] = g[:, cols]
        gt[:, lanes] = g[:, cols].T
    device = lax.axis_index(AXES[0]) * lax.axis_size(AXES[1]) + lax.axis_index(AXES[1])
    here = device * rows
    later = lax.broadcasted_iota(jnp.int32, (docs, docs), 0)
    earlier = lax.broadcasted_iota(jnp.int32, (docs, docs), 1)
    counted = jnp.where(earlier <= later, lengths[...].astype(jnp.float32), 0.0)
    ends = jnp.sum(counted, axis=1, keepdims=True)
    pos = (lax.broadcasted_iota(jnp.int32, (docs, rows), 1) + here).astype(jnp.float32)
    start = jnp.max(jnp.where(ends <= pos, ends, 0.0), axis=0, keepdims=True)
    meta[0:1, :] = start.astype(jnp.int32) - here
    meta[1:2, :] = jnp.full((1, rows), device % 2, jnp.int32)


def stack(queries, grad, lengths, dim):
    rows, wide = queries.shape
    tall = jax.ShapeDtypeStruct((rows * wide // dim, dim), queries.dtype)
    return pl.pallas_call(
        stack_body,
        in_specs=[HERE] * 3,
        out_specs=[HERE] * 4,
        out_shape=[
            tall,
            tall,
            jax.ShapeDtypeStruct(tall.shape[::-1], queries.dtype),
            jax.ShapeDtypeStruct((2, rows), jnp.int32),
        ],
        compiler_params=pltpu.CompilerParams(vmem_limit_bytes=VMEM_LIMIT),
    )(queries, grad, lengths)


def stage_body(plan, *refs):
    rows, dim, heads = plan["rows"], plan["dim"], plan["heads"]
    fwd, bwd = plan["fwd"], plan["bwd"]
    ref = dict(zip(plan["names"], refs))
    fold = math.log2(math.e) / math.sqrt(dim)
    scale = 1.0 / math.sqrt(dim)
    bf16, f32 = jnp.bfloat16, jnp.float32
    meta = ref["meta"]
    start = meta[0:1, :]
    earliest = jnp.min(start)
    odd = jnp.max(meta[1:2, :])
    blocks = sorted(set(fwd) | set(bwd))
    cols = [slice(h * dim, (h + 1) * dim) for h in range(heads)]
    lanes = [slice(h * rows, (h + 1) * rows) for h in range(heads)]

    def place(chip, side):
        return (side * (1 - 2 * odd) - 2 * chip) * rows

    def needed(chip, side):
        return (place(chip, side) + rows > earliest) & (place(chip, side) <= 0)

    if plan["first"]:
        ref["m"][...] = jnp.full_like(ref["m"], MASKED)
        ref["l"][...] = jnp.zeros_like(ref["l"])
        ref["acc"][...] = jnp.zeros_like(ref["acc"])

    def load(chip, side):
        block, i = ref["kv", chip, side], blocks.index((chip, side))
        if (chip, side) in fwd:
            ref["vt"][i] = block[:, dim:].T
        if (chip, side) in bwd:
            ref["kt"][i] = block[:, :dim].T

    for block in blocks:
        pl.when(needed(*block))(functools.partial(load, *block))

    def fwd_block(chip, side):
        i = blocks.index((chip, side))
        key_pos = lax.broadcasted_iota(jnp.int32, (rows, rows), 0) + place(chip, side)
        allowed = (key_pos >= start) & (
            key_pos <= lax.broadcasted_iota(jnp.int32, (rows, rows), 1)
        )
        ref["bias"][...] = jnp.where(allowed, 0.0, MASKED)
        block_k, value_t = ref["kv", chip, side][:, :dim], ref["vt"][i]
        for h in range(0, heads, 8):
            wide = slice(h * rows, (h + 8) * rows)
            s = dot_nt(block_k, ref["qs"][wide, :]) + jnp.concatenate([ref["bias"][...]] * 8, axis=1)
            old = ref["m"][:, wide]
            m = jnp.maximum(old, jnp.max(s, axis=0, keepdims=True))
            alpha = jnp.exp2((old - m) * fold)
            p = jnp.exp2((s - m) * fold)
            pb = p.astype(bf16)
            ref["probs", chip, side][:, wide] = pb
            total = jnp.sum(p, axis=0, keepdims=True)
            ref["l"][:, wide] = ref["l"][:, wide] * alpha + total
            ref["acc"][:, wide] = ref["acc"][:, wide] * alpha + dot_nn(value_t, pb)
            ref["m"][:, wide] = m
            ref["then", chip, side][:, wide] = m

    def finish():
        for h in range(heads):
            inverse = 1.0 / ref["l"][:, lanes[h]]
            o_t = (ref["acc"][:, lanes[h]] * inverse).astype(bf16)
            ref["out_t"][:, lanes[h]] = o_t
            terms = o_t.astype(f32) * ref["gt"][:, lanes[h]].astype(f32)
            ref["delta"][:, lanes[h]] = jnp.sum(terms, axis=0, keepdims=True)
            ref["l"][:, lanes[h]] = inverse
        ref["dq"][...] = jnp.zeros_like(ref["dq"])

    def bwd_block(chip, side):
        i = blocks.index((chip, side))
        block_v, key_t = ref["kv", chip, side][:, dim:], ref["kt"][i]
        dk = dv = None
        for h in range(0, heads, 8):
            wide = slice(h * rows, (h + 8) * rows)
            dprob = dot_nn(block_v, ref["gt"][:, wide])
            m_then = ref["then", chip, side][:, wide]
            c = jnp.exp2((m_then - ref["m"][:, wide]) * fold) * ref["l"][:, wide]
            p = ref["probs", chip, side][:, wide].astype(f32) * c
            d = (p * (dprob - ref["delta"][:, wide])).astype(bf16)
            p = p.astype(bf16)
            ref["dq"][:, wide] += dot_nn(key_t, d)
            dk_part = dot_nn(d, ref["qs"][wide, :])
            dv_part = dot_nn(p, ref["gs"][wide, :])
            dk = dk_part if dk is None else dk + dk_part
            dv = dv_part if dv is None else dv + dv_part
        part = ref["part", chip, side]
        part[:, :dim] = (dk * scale).astype(part.dtype)
        part[:, dim:] = dv.astype(part.dtype)

    for block in fwd:
        pl.when(needed(*block))(functools.partial(fwd_block, *block))
    if plan["final"]:
        finish()
    for block in bwd:
        part = ref["part", *block]
        pl.when(needed(*block))(functools.partial(bwd_block, *block))

        @pl.when(jnp.logical_not(needed(*block)))
        def _():
            part[...] = jnp.zeros_like(part)

    if plan["last"]:
        for h in range(heads):
            ref["out"][:, cols[h]] = ref["out_t"][:, lanes[h]].T
            ref["grad_q"][:, cols[h]] = (ref["dq"][:, lanes[h]] * scale).astype(bf16).T


def stage(state, fwd=(), bwd=(), final=False, last=False):
    rows, dim2 = state["kv", 0, 0].shape
    dim = dim2 // 2
    width = state["qs"].shape[0]
    heads = width // rows
    bf16, f32 = jnp.bfloat16, jnp.float32
    shape = jax.ShapeDtypeStruct
    blocks = sorted(set(fwd) | set(bwd))
    first = (0, 0) in fwd
    row, tall = shape((1, width), f32), shape((dim, width), f32)
    ins, outs, both = ["meta", "qs"], {}, []
    if final or bwd:
        ins.append("gt")
    if bwd:
        ins.append("gs")
    ins += [("kv", *b) for b in blocks]
    if fwd:
        for b in fwd:
            outs["probs", *b] = shape((rows, width), bf16)
            outs["then", *b] = row
        outs.update(m=row, l=row, acc=tall)
        if not first:
            both += ["m", "l", "acc"]
    if final:
        outs.update(out_t=shape((dim, width), bf16), delta=row, dq=tall)
    if bwd:
        for b in bwd:
            if b not in fwd:
                ins += [("probs", *b), ("then", *b)]
            outs["part", *b] = shape((rows, dim2), bf16 if b[1] else f32)
        if not final:
            ins += ["m", "l", "delta"]
            outs["dq"] = tall
            both.append("dq")
    if last:
        ins.append("out_t")
        outs["out"] = outs["grad_q"] = shape((rows, heads * dim), bf16)
    out_names = list(outs)
    scratch = {}
    if fwd:
        scratch["vt"] = pltpu.VMEM((len(blocks), dim, rows), bf16)
        scratch["bias"] = pltpu.VMEM((rows, rows), f32)
    if bwd:
        scratch["kt"] = pltpu.VMEM((len(blocks), dim, rows), bf16)
    names = ins + [("in", b) for b in both] + out_names + list(scratch)
    plan = dict(
        rows=rows, dim=dim, heads=heads, fwd=fwd, bwd=bwd, first=first, final=final, last=last, names=names
    )
    results = pl.pallas_call(
        functools.partial(stage_body, plan),
        in_specs=[HERE] * (len(ins) + len(both)),
        out_specs=[HERE] * len(out_names),
        out_shape=[outs[n] for n in out_names],
        scratch_shapes=list(scratch.values()),
        input_output_aliases={len(ins) + i: out_names.index(b) for i, b in enumerate(both)},
        compiler_params=pltpu.CompilerParams(vmem_limit_bytes=VMEM_LIMIT),
        cost_estimate=QUICK,
    )(*[state[n] for n in ins + both])
    state.update(zip(out_names, results))


def after(x, *others):
    return lax.optimization_barrier((x, *others))[0]


def pairs(*chips):
    return [(chip, side) for chip in chips for side in (0, 1)]


def on_device(queries, keys, values, out_grad, doc_lengths):
    rows, dim = keys.shape
    f32, bf16 = jnp.float32, jnp.bfloat16
    own = beside(keys, values)
    state = dict(zip(("qs", "gs", "gt", "meta"), stack(queries, out_grad, doc_lengths[None, :], dim)))

    back2 = shifted(own, 4)
    back1 = shifted(own, 2)
    back2 = after(back2, state["qs"])
    back4 = shifted(back2, 4)
    back3 = shifted(back2, 2)
    state["kv", 0, 0], state["kv", 0, 1] = own, swapped(own)
    state["kv", 1, 0] = back1
    state["kv", 2, 0], state["kv", 2, 1] = back2, swapped(back2)
    stage(state, fwd=pairs(0, 2) + [(1, 0)])
    state["kv", 1, 1] = swapped(after(back1, state["l"]))
    for chip, block in ((3, back3), (4, back4)):
        block = after(block, state["l"])
        state["kv", chip, 0], state["kv", chip, 1] = block, swapped(block)
    stage(state, fwd=[(3, 0), (4, 0)])
    stage(state, fwd=[(1, 1), (3, 1), (4, 1)], bwd=[(3, 1), (4, 1)], final=True)
    stage(state, bwd=[(4, 0)])

    def summed(chip, *others):
        other = swapped(after(state["part", chip, 1], *others))
        return state["part", chip, 0] + other.astype(f32), other

    t4, swap4 = summed(4)
    t4 = t4.astype(bf16)
    state["dq"] = after(state["dq"], t4)
    stage(state, bwd=[(3, 0)])
    t3, _ = summed(3, swap4)
    t3 = t3.astype(bf16)
    r4, r3 = shifted(t4, -4), shifted(t3, -2)
    state["dq"] = after(state["dq"], t3, t4)
    stage(state, bwd=pairs(1, 2) + [(0, 1)])
    t2, swap2 = summed(2, r3, r4)
    t2 = (t2 + r4.astype(f32) + r3.astype(f32)).astype(bf16)
    t1, _ = summed(1, swap2)
    t1 = t1.astype(bf16)
    r2, r1 = shifted(t2, -4), shifted(t1, -2)
    other = swapped(after(state["part", 0, 1], swap2))
    state["dq"] = after(state["dq"], t1, t2)
    stage(state, bwd=[(0, 0)], last=True)
    total = state["part", 0, 0] + other.astype(f32) + r1.astype(f32) + r2.astype(f32)
    return (state["out"], state["grad_q"], total[:, :dim].astype(bf16), total[:, dim:].astype(bf16))


def solution(mesh):
    rows = P(AXES, None)
    return jax.shard_map(
        on_device,
        mesh=mesh,
        in_specs=(rows, rows, rows, rows, P()),
        out_specs=(rows, rows, rows, rows),
        check_vma=False,
    )
```

```python
import functools
import math

import jax
import jax.numpy as jnp
from jax import lax
from jax.experimental import pallas as pl
from jax.experimental.pallas import tpu as pltpu
from jax.sharding import PartitionSpec as P

AXES = ("node", "wide")
MASKED = -1e30
VMEM_LIMIT = 16 * 1024 * 1024
QUICK = pl.CostEstimate(flops=1, bytes_accessed=1, transcendentals=0)
HERE = pl.BlockSpec(memory_space=pltpu.VMEM)


def shifted(shard, by):
    peers = lax.axis_size(AXES)
    pairs = [(i, i + by) for i in range(peers) if 0 <= i + by < peers]
    return lax.ppermute(shard, AXES, pairs)


def swapped(shard):
    peers = lax.axis_size(AXES)
    return lax.ppermute(shard, AXES, [(i, i ^ 1) for i in range(peers)])


def dot_nt(a, b):
    return lax.dot_general(a, b, (((1,), (1,)), ((), ())), preferred_element_type=jnp.float32)


def dot_nn(a, b):
    return lax.dot_general(a, b, (((1,), (0,)), ((), ())), preferred_element_type=jnp.float32)


def beside(keys, values):
    dim = keys.shape[1]
    lane = lax.broadcasted_iota(jnp.int32, (keys.shape[0], 2 * dim), 1)
    none = jnp.zeros((), keys.dtype)
    left = lax.pad(keys, none, ((0, 0, 0), (0, dim, 0)))
    right = lax.pad(values, none, ((0, 0, 0), (dim, 0, 0)))
    return jnp.where(lane < dim, left, right)


def stack_body(q, g, lengths, qs, gs, gt, meta):
    rows, dim = q.shape[0], qs.shape[1]
    docs = lengths.shape[1]
    for h in range(q.shape[1] // dim):
        cols, lanes = slice(h * dim, (h + 1) * dim), slice(h * rows, (h + 1) * rows)
        qs[lanes, :] = q[:, cols]
        gs[lanes, :] = g[:, cols]
        gt[:, lanes] = g[:, cols].T
    device = lax.axis_index(AXES[0]) * lax.axis_size(AXES[1]) + lax.axis_index(AXES[1])
    here = device * rows
    later = lax.broadcasted_iota(jnp.int32, (docs, docs), 0)
    earlier = lax.broadcasted_iota(jnp.int32, (docs, docs), 1)
    counted = jnp.where(earlier <= later, lengths[...].astype(jnp.float32), 0.0)
    ends = jnp.sum(counted, axis=1, keepdims=True)
    pos = (lax.broadcasted_iota(jnp.int32, (docs, rows), 1) + here).astype(jnp.float32)
    start = jnp.max(jnp.where(ends <= pos, ends, 0.0), axis=0, keepdims=True)
    meta[0:1, :] = start.astype(jnp.int32) - here
    meta[1:2, :] = jnp.full((1, rows), device % 2, jnp.int32)


def stack(queries, grad, lengths, dim):
    rows, wide = queries.shape
    tall = jax.ShapeDtypeStruct((rows * wide // dim, dim), queries.dtype)
    return pl.pallas_call(
        stack_body,
        in_specs=[HERE] * 3,
        out_specs=[HERE] * 4,
        out_shape=[
            tall,
            tall,
            jax.ShapeDtypeStruct(tall.shape[::-1], queries.dtype),
            jax.ShapeDtypeStruct((2, rows), jnp.int32),
        ],
        compiler_params=pltpu.CompilerParams(vmem_limit_bytes=VMEM_LIMIT),
    )(queries, grad, lengths)


def stage_body(plan, *refs):
    rows, dim, heads = plan["rows"], plan["dim"], plan["heads"]
    fwd, bwd = plan["fwd"], plan["bwd"]
    ref = dict(zip(plan["names"], refs))
    fold = math.log2(math.e) / math.sqrt(dim)
    scale = 1.0 / math.sqrt(dim)
    bf16, f32 = jnp.bfloat16, jnp.float32
    meta = ref["meta"]
    start = meta[0:1, :]
    earliest = jnp.min(start)
    odd = jnp.max(meta[1:2, :])
    blocks = sorted(set(fwd) | set(bwd))
    cols = [slice(h * dim, (h + 1) * dim) for h in range(heads)]
    lanes = [slice(h * rows, (h + 1) * rows) for h in range(heads)]

    def place(chip, side):
        return (side * (1 - 2 * odd) - 2 * chip) * rows

    def needed(chip, side):
        return (place(chip, side) + rows > earliest) & (place(chip, side) <= 0)

    if plan["first"]:
        ref["m"][...] = jnp.full_like(ref["m"], MASKED)
        ref["l"][...] = jnp.zeros_like(ref["l"])
        ref["acc"][...] = jnp.zeros_like(ref["acc"])

    def load(chip, side):
        block, i = ref["kv", chip, side], blocks.index((chip, side))
        if (chip, side) in fwd:
            ref["vt"][i] = block[:, dim:].T
        if (chip, side) in bwd:
            ref["kt"][i] = block[:, :dim].T

    for block in blocks:
        pl.when(needed(*block))(functools.partial(load, *block))

    def fwd_block(chip, side):
        i = blocks.index((chip, side))
        key_pos = lax.broadcasted_iota(jnp.int32, (rows, rows), 0) + place(chip, side)
        allowed = (key_pos >= start) & (
            key_pos <= lax.broadcasted_iota(jnp.int32, (rows, rows), 1)
        )
        ref["bias"][...] = jnp.where(allowed, 0.0, MASKED)
        block_k, value_t = ref["kv", chip, side][:, :dim], ref["vt"][i]
        for h in range(0, heads, 8):
            wide = slice(h * rows, (h + 8) * rows)
            s = dot_nt(block_k, ref["qs"][wide, :]) + jnp.concatenate([ref["bias"][...]] * 8, axis=1)
            old = ref["m"][:, wide]
            m = jnp.maximum(old, jnp.max(s, axis=0, keepdims=True))
            alpha = jnp.exp2((old - m) * fold)
            p = jnp.exp2((s - m) * fold)
            pb = p.astype(bf16)
            ref["probs", chip, side][:, wide] = pb
            total = jnp.sum(p, axis=0, keepdims=True)
            ref["l"][:, wide] = ref["l"][:, wide] * alpha + total
            ref["acc"][:, wide] = ref["acc"][:, wide] * alpha + dot_nn(value_t, pb)
            ref["m"][:, wide] = m
            ref["then", chip, side][:, wide] = m

    def finish():
        inverse = 1.0 / ref["l"][...]
        o_t = (ref["acc"][...] * inverse).astype(bf16)
        ref["out_t"][...] = o_t
        terms = o_t.astype(f32) * ref["gt"][...].astype(f32)
        ref["delta"][...] = jnp.sum(terms, axis=0, keepdims=True)
        ref["l"][...] = inverse
        ref["dq"][...] = jnp.zeros_like(ref["dq"])

    def bwd_block(chip, side):
        i = blocks.index((chip, side))
        block_v, key_t = ref["kv", chip, side][:, dim:], ref["kt"][i]
        dk = dv = None
        for h in range(0, heads, 8):
            wide = slice(h * rows, (h + 8) * rows)
            dprob = dot_nn(block_v, ref["gt"][:, wide])
            m_then = ref["then", chip, side][:, wide]
            c = jnp.exp2((m_then - ref["m"][:, wide]) * fold) * ref["l"][:, wide]
            p = ref["probs", chip, side][:, wide].astype(f32) * c
            d = (p * (dprob - ref["delta"][:, wide])).astype(bf16)
            p = p.astype(bf16)
            ref["dq"][:, wide] += dot_nn(key_t, d)
            dk_part = dot_nn(d, ref["qs"][wide, :])
            dv_part = dot_nn(p, ref["gs"][wide, :])
            dk = dk_part if dk is None else dk + dk_part
            dv = dv_part if dv is None else dv + dv_part
        part = ref["part", chip, side]
        part[:, :dim] = (dk * scale).astype(part.dtype)
        part[:, dim:] = dv.astype(part.dtype)

    for block in fwd:
        pl.when(needed(*block))(functools.partial(fwd_block, *block))
    if plan["final"]:
        finish()
    for block in bwd:
        part = ref["part", *block]
        pl.when(needed(*block))(functools.partial(bwd_block, *block))

        @pl.when(jnp.logical_not(needed(*block)))
        def _():
            part[...] = jnp.zeros_like(part)

    if plan["last"]:
        for h in range(heads):
            ref["out"][:, cols[h]] = ref["out_t"][:, lanes[h]].T
            ref["grad_q"][:, cols[h]] = (ref["dq"][:, lanes[h]] * scale).astype(bf16).T


def stage(state, fwd=(), bwd=(), final=False, last=False):
    rows, dim2 = state["kv", 0, 0].shape
    dim = dim2 // 2
    width = state["qs"].shape[0]
    heads = width // rows
    bf16, f32 = jnp.bfloat16, jnp.float32
    shape = jax.ShapeDtypeStruct
    blocks = sorted(set(fwd) | set(bwd))
    first = (0, 0) in fwd
    row, tall = shape((1, width), f32), shape((dim, width), f32)
    ins, outs, both = ["meta", "qs"], {}, []
    if final or bwd:
        ins.append("gt")
    if bwd:
        ins.append("gs")
    ins += [("kv", *b) for b in blocks]
    if fwd:
        for b in fwd:
            outs["probs", *b] = shape((rows, width), bf16)
            outs["then", *b] = row
        outs.update(m=row, l=row, acc=tall)
        if not first:
            both += ["m", "l", "acc"]
    if final:
        outs.update(out_t=shape((dim, width), bf16), delta=row, dq=tall)
    if bwd:
        for b in bwd:
            if b not in fwd:
                ins += [("probs", *b), ("then", *b)]
            outs["part", *b] = shape((rows, dim2), bf16 if b[1] else f32)
        if not final:
            ins += ["m", "l", "delta"]
            outs["dq"] = tall
            both.append("dq")
    if last:
        ins.append("out_t")
        outs["out"] = outs["grad_q"] = shape((rows, heads * dim), bf16)
    out_names = list(outs)
    scratch = {}
    if fwd:
        scratch["vt"] = pltpu.VMEM((len(blocks), dim, rows), bf16)
        scratch["bias"] = pltpu.VMEM((rows, rows), f32)
    if bwd:
        scratch["kt"] = pltpu.VMEM((len(blocks), dim, rows), bf16)
    names = ins + [("in", b) for b in both] + out_names + list(scratch)
    plan = dict(
        rows=rows, dim=dim, heads=heads, fwd=fwd, bwd=bwd, first=first, final=final, last=last, names=names
    )
    results = pl.pallas_call(
        functools.partial(stage_body, plan),
        in_specs=[HERE] * (len(ins) + len(both)),
        out_specs=[HERE] * len(out_names),
        out_shape=[outs[n] for n in out_names],
        scratch_shapes=list(scratch.values()),
        input_output_aliases={len(ins) + i: out_names.index(b) for i, b in enumerate(both)},
        compiler_params=pltpu.CompilerParams(vmem_limit_bytes=VMEM_LIMIT),
        cost_estimate=QUICK,
    )(*[state[n] for n in ins + both])
    state.update(zip(out_names, results))


def after(x, *others):
    return lax.optimization_barrier((x, *others))[0]


def pairs(*chips):
    return [(chip, side) for chip in chips for side in (0, 1)]


def on_device(queries, keys, values, out_grad, doc_lengths):
    rows, dim = keys.shape
    f32, bf16 = jnp.float32, jnp.bfloat16
    own = beside(keys, values)
    state = dict(zip(("qs", "gs", "gt", "meta"), stack(queries, out_grad, doc_lengths[None, :], dim)))

    back2 = shifted(own, 4)
    back1 = shifted(after(own, state["qs"]), 2)
    back2 = after(back2, state["qs"])
    back4 = shifted(back2, 4)
    back3 = shifted(back2, 2)
    state["kv", 0, 0], state["kv", 0, 1] = own, swapped(own)
    state["kv", 1, 0] = back1
    state["kv", 2, 0], state["kv", 2, 1] = back2, swapped(back2)
    stage(state, fwd=pairs(0, 2) + [(1, 0)])
    state["kv", 1, 1] = swapped(after(back1, state["l"]))
    for chip, block in ((3, back3), (4, back4)):
        block = after(block, state["l"])
        state["kv", chip, 0], state["kv", chip, 1] = block, swapped(block)
    stage(state, fwd=[(3, 0), (4, 0)])
    stage(state, fwd=[(1, 1), (3, 1), (4, 1)], bwd=[(3, 1), (4, 1)], final=True)
    stage(state, bwd=[(4, 0)])

    def summed(chip, *others):
        other = swapped(after(state["part", chip, 1], *others))
        return state["part", chip, 0] + other.astype(f32), other

    t4, swap4 = summed(4)
    t4 = t4.astype(bf16)
    state["dq"] = after(state["dq"], t4)
    stage(state, bwd=[(3, 0)])
    t3, _ = summed(3, swap4)
    t3 = t3.astype(bf16)
    r4, r3 = shifted(t4, -4), shifted(t3, -2)
    state["dq"] = after(state["dq"], t3, t4)
    stage(state, bwd=pairs(1, 2) + [(0, 1)])
    t2, swap2 = summed(2, r3, r4)
    t2 = (t2 + r4.astype(f32) + r3.astype(f32)).astype(bf16)
    t1, _ = summed(1, swap2)
    t1 = t1.astype(bf16)
    r2, r1 = shifted(t2, -4), shifted(t1, -2)
    other = swapped(after(state["part", 0, 1], swap2))
    state["dq"] = after(state["dq"], t1, t2)
    stage(state, bwd=[(0, 0)], last=True)
    total = state["part", 0, 0] + other.astype(f32) + r1.astype(f32) + r2.astype(f32)
    return (state["out"], state["grad_q"], total[:, :dim].astype(bf16), total[:, dim:].astype(bf16))


def solution(mesh):
    rows = P(AXES, None)
    return jax.shard_map(
        on_device,
        mesh=mesh,
        in_specs=(rows, rows, rows, rows, P()),
        out_specs=(rows, rows, rows, rows),
        check_vma=False,
    )
```

```python
import functools
import math

import jax
import jax.numpy as jnp
from jax import lax
from jax.experimental import pallas as pl
from jax.experimental.pallas import tpu as pltpu
from jax.sharding import PartitionSpec as P

AXES = ("node", "wide")
MASKED = -1e30
VMEM_LIMIT = 16 * 1024 * 1024
QUICK = pl.CostEstimate(flops=1, bytes_accessed=1, transcendentals=0)
HERE = pl.BlockSpec(memory_space=pltpu.VMEM)


def shifted(shard, by):
    peers = lax.axis_size(AXES)
    pairs = [(i, i + by) for i in range(peers) if 0 <= i + by < peers]
    return lax.ppermute(shard, AXES, pairs)


def swapped(shard):
    peers = lax.axis_size(AXES)
    return lax.ppermute(shard, AXES, [(i, i ^ 1) for i in range(peers)])


def dot_nt(a, b):
    return lax.dot_general(a, b, (((1,), (1,)), ((), ())), preferred_element_type=jnp.float32)


def dot_nn(a, b):
    return lax.dot_general(a, b, (((1,), (0,)), ((), ())), preferred_element_type=jnp.float32)


def beside(keys, values):
    dim = keys.shape[1]
    lane = lax.broadcasted_iota(jnp.int32, (keys.shape[0], 2 * dim), 1)
    none = jnp.zeros((), keys.dtype)
    left = lax.pad(keys, none, ((0, 0, 0), (0, dim, 0)))
    right = lax.pad(values, none, ((0, 0, 0), (dim, 0, 0)))
    return jnp.where(lane < dim, left, right)


def stack_body(q, g, lengths, qs, gs, gt, meta):
    rows, dim = q.shape[0], qs.shape[1]
    docs = lengths.shape[1]
    for h in range(q.shape[1] // dim):
        cols, lanes = slice(h * dim, (h + 1) * dim), slice(h * rows, (h + 1) * rows)
        qs[lanes, :] = q[:, cols]
        gs[lanes, :] = g[:, cols]
        gt[:, lanes] = g[:, cols].T
    device = lax.axis_index(AXES[0]) * lax.axis_size(AXES[1]) + lax.axis_index(AXES[1])
    here = device * rows
    later = lax.broadcasted_iota(jnp.int32, (docs, docs), 0)
    earlier = lax.broadcasted_iota(jnp.int32, (docs, docs), 1)
    counted = jnp.where(earlier <= later, lengths[...].astype(jnp.float32), 0.0)
    ends = jnp.sum(counted, axis=1, keepdims=True)
    pos = (lax.broadcasted_iota(jnp.int32, (docs, rows), 1) + here).astype(jnp.float32)
    start = jnp.max(jnp.where(ends <= pos, ends, 0.0), axis=0, keepdims=True)
    meta[0:1, :] = start.astype(jnp.int32) - here
    meta[1:2, :] = jnp.full((1, rows), device % 2, jnp.int32)


def stack(queries, grad, lengths, dim):
    rows, wide = queries.shape
    tall = jax.ShapeDtypeStruct((rows * wide // dim, dim), queries.dtype)
    return pl.pallas_call(
        stack_body,
        in_specs=[HERE] * 3,
        out_specs=[HERE] * 4,
        out_shape=[
            tall,
            tall,
            jax.ShapeDtypeStruct(tall.shape[::-1], queries.dtype),
            jax.ShapeDtypeStruct((2, rows), jnp.int32),
        ],
        compiler_params=pltpu.CompilerParams(vmem_limit_bytes=VMEM_LIMIT),
    )(queries, grad, lengths)


def stage_body(plan, *refs):
    rows, dim, heads = plan["rows"], plan["dim"], plan["heads"]
    fwd, bwd = plan["fwd"], plan["bwd"]
    ref = dict(zip(plan["names"], refs))
    fold = math.log2(math.e) / math.sqrt(dim)
    scale = 1.0 / math.sqrt(dim)
    bf16, f32 = jnp.bfloat16, jnp.float32
    meta = ref["meta"]
    start = meta[0:1, :]
    earliest = jnp.min(start)
    odd = jnp.max(meta[1:2, :])
    blocks = sorted(set(fwd) | set(bwd))
    cols = [slice(h * dim, (h + 1) * dim) for h in range(heads)]
    lanes = [slice(h * rows, (h + 1) * rows) for h in range(heads)]

    def place(chip, side):
        return (side * (1 - 2 * odd) - 2 * chip) * rows

    def needed(chip, side):
        return (place(chip, side) + rows > earliest) & (place(chip, side) <= 0)

    if plan["first"]:
        ref["m"][...] = jnp.full_like(ref["m"], MASKED)
        ref["l"][...] = jnp.zeros_like(ref["l"])
        ref["acc"][...] = jnp.zeros_like(ref["acc"])

    def load(chip, side):
        block, i = ref["kv", chip, side], blocks.index((chip, side))
        if (chip, side) in fwd:
            ref["vt"][i] = block[:, dim:].T
        if (chip, side) in bwd:
            ref["kt"][i] = block[:, :dim].T

    for block in blocks:
        pl.when(needed(*block))(functools.partial(load, *block))

    def fwd_block(chip, side):
        i = blocks.index((chip, side))
        key_pos = lax.broadcasted_iota(jnp.int32, (rows, rows), 0) + place(chip, side)
        allowed = (key_pos >= start) & (
            key_pos <= lax.broadcasted_iota(jnp.int32, (rows, rows), 1)
        )
        ref["bias"][...] = jnp.where(allowed, 0.0, MASKED)
        block_k, value_t = ref["kv", chip, side][:, :dim], ref["vt"][i]
        for h in range(0, heads, 8):
            wide = slice(h * rows, (h + 8) * rows)
            s = dot_nt(block_k, ref["qs"][wide, :]) + jnp.concatenate([ref["bias"][...]] * 8, axis=1)
            old = ref["m"][:, wide]
            m = jnp.maximum(old, jnp.max(s, axis=0, keepdims=True))
            alpha = jnp.exp2((old - m) * fold)
            p = jnp.exp2((s - m) * fold)
            pb = p.astype(bf16)
            ref["probs", chip, side][:, wide] = pb
            total = jnp.sum(p, axis=0, keepdims=True)
            ref["l"][:, wide] = ref["l"][:, wide] * alpha + total
            ref["acc"][:, wide] = ref["acc"][:, wide] * alpha + dot_nn(value_t, pb)
            ref["m"][:, wide] = m
            ref["then", chip, side][:, wide] = m

    def finish():
        inverse = 1.0 / ref["l"][...]
        o_t = (ref["acc"][...] * inverse).astype(bf16)
        ref["out_t"][...] = o_t
        terms = o_t.astype(f32) * ref["gt"][...].astype(f32)
        ref["delta"][...] = jnp.sum(terms, axis=0, keepdims=True)
        ref["l"][...] = inverse
        ref["dq"][...] = jnp.zeros_like(ref["dq"])

    def bwd_block(chip, side):
        i = blocks.index((chip, side))
        block_v, key_t = ref["kv", chip, side][:, dim:], ref["kt"][i]
        dk = dv = None
        for h in range(0, heads, 8):
            wide = slice(h * rows, (h + 8) * rows)
            dprob = dot_nn(block_v, ref["gt"][:, wide])
            m_then = ref["then", chip, side][:, wide]
            c = jnp.exp2((m_then - ref["m"][:, wide]) * fold) * ref["l"][:, wide]
            p = ref["probs", chip, side][:, wide].astype(f32) * c
            d = (p * (dprob - ref["delta"][:, wide])).astype(bf16)
            p = p.astype(bf16)
            ref["dq"][:, wide] += dot_nn(key_t, d)
            dk_part = dot_nn(d, ref["qs"][wide, :])
            dv_part = dot_nn(p, ref["gs"][wide, :])
            dk = dk_part if dk is None else dk + dk_part
            dv = dv_part if dv is None else dv + dv_part
        part = ref["part", chip, side]
        part[:, :dim] = (dk * scale).astype(part.dtype)
        part[:, dim:] = dv.astype(part.dtype)

    for block in fwd:
        pl.when(needed(*block))(functools.partial(fwd_block, *block))
    if plan["final"]:
        finish()
    for block in bwd:
        part = ref["part", *block]
        pl.when(needed(*block))(functools.partial(bwd_block, *block))

        @pl.when(jnp.logical_not(needed(*block)))
        def _():
            part[...] = jnp.zeros_like(part)

    if plan["last"]:
        for h in range(heads):
            ref["out"][:, cols[h]] = ref["out_t"][:, lanes[h]].T
            ref["grad_q"][:, cols[h]] = (ref["dq"][:, lanes[h]] * scale).astype(bf16).T


def stage(state, fwd=(), bwd=(), final=False, last=False):
    rows, dim2 = state["kv", 0, 0].shape
    dim = dim2 // 2
    width = state["qs"].shape[0]
    heads = width // rows
    bf16, f32 = jnp.bfloat16, jnp.float32
    shape = jax.ShapeDtypeStruct
    blocks = sorted(set(fwd) | set(bwd))
    first = (0, 0) in fwd
    row, tall = shape((1, width), f32), shape((dim, width), f32)
    ins, outs, both = ["meta", "qs"], {}, []
    if final or bwd:
        ins.append("gt")
    if bwd:
        ins.append("gs")
    ins += [("kv", *b) for b in blocks]
    if fwd:
        for b in fwd:
            outs["probs", *b] = shape((rows, width), bf16)
            outs["then", *b] = row
        outs.update(m=row, l=row, acc=tall)
        if not first:
            both += ["m", "l", "acc"]
    if final:
        outs.update(out_t=shape((dim, width), bf16), delta=row, dq=tall)
    if bwd:
        for b in bwd:
            if b not in fwd:
                ins += [("probs", *b), ("then", *b)]
            outs["part", *b] = shape((rows, dim2), bf16 if b[1] else f32)
        if not final:
            ins += ["m", "l", "delta"]
            outs["dq"] = tall
            both.append("dq")
    if last:
        ins.append("out_t")
        outs["out"] = outs["grad_q"] = shape((rows, heads * dim), bf16)
    out_names = list(outs)
    scratch = {}
    if fwd:
        scratch["vt"] = pltpu.VMEM((len(blocks), dim, rows), bf16)
        scratch["bias"] = pltpu.VMEM((rows, rows), f32)
    if bwd:
        scratch["kt"] = pltpu.VMEM((len(blocks), dim, rows), bf16)
    names = ins + [("in", b) for b in both] + out_names + list(scratch)
    plan = dict(
        rows=rows, dim=dim, heads=heads, fwd=fwd, bwd=bwd, first=first, final=final, last=last, names=names
    )
    results = pl.pallas_call(
        functools.partial(stage_body, plan),
        in_specs=[HERE] * (len(ins) + len(both)),
        out_specs=[HERE] * len(out_names),
        out_shape=[outs[n] for n in out_names],
        scratch_shapes=list(scratch.values()),
        input_output_aliases={len(ins) + i: out_names.index(b) for i, b in enumerate(both)},
        compiler_params=pltpu.CompilerParams(vmem_limit_bytes=VMEM_LIMIT),
        cost_estimate=QUICK,
    )(*[state[n] for n in ins + both])
    state.update(zip(out_names, results))


def after(x, *others):
    return lax.optimization_barrier((x, *others))[0]


def pairs(*chips):
    return [(chip, side) for chip in chips for side in (0, 1)]


def on_device(queries, keys, values, out_grad, doc_lengths):
    rows, dim = keys.shape
    f32, bf16 = jnp.float32, jnp.bfloat16
    own = beside(keys, values)
    state = dict(zip(("qs", "gs", "gt", "meta"), stack(queries, out_grad, doc_lengths[None, :], dim)))

    back2 = shifted(own, 4)
    back1 = shifted(after(own, state["qs"]), 2)
    back2 = after(back2, state["qs"])
    back4 = shifted(back2, 4)
    back3 = shifted(back2, 2)
    state["kv", 0, 0], state["kv", 0, 1] = own, swapped(own)
    state["kv", 1, 0] = back1
    state["kv", 2, 0], state["kv", 2, 1] = back2, swapped(back2)
    stage(state, fwd=pairs(0, 2) + [(1, 0)])
    state["kv", 1, 1] = swapped(after(back1, state["l"]))
    for chip, block in ((3, back3), (4, back4)):
        block = after(block, state["l"])
        state["kv", chip, 0], state["kv", chip, 1] = block, swapped(block)
    stage(state, fwd=[(3, 0), (4, 0)])
    stage(state, fwd=[(1, 1), (3, 1), (4, 1)], bwd=[(3, 1), (4, 1)], final=True)
    stage(state, bwd=[(4, 0)])

    def summed(chip, *others):
        other = swapped(after(state["part", chip, 1], *others))
        return state["part", chip, 0] + other.astype(f32), other

    t4, swap4 = summed(4)
    t4 = t4.astype(bf16)
    state["dq"] = after(state["dq"], t4)
    stage(state, bwd=[(3, 0)])
    t3, _ = summed(3, swap4)
    t3 = t3.astype(bf16)
    r4, r3 = shifted(t4, -4), shifted(t3, -2)
    state["dq"] = after(state["dq"], t3, t4)
    stage(state, bwd=pairs(2) + [(1, 1)])
    t2, swap2 = summed(2, r3, r4)
    t2 = (t2 + r4.astype(f32) + r3.astype(f32)).astype(bf16)
    r2 = shifted(t2, -4)
    state["dq"] = after(state["dq"], t2)
    stage(state, bwd=[(1, 0), (0, 1)])
    t1, swap1 = summed(1, swap2)
    t1 = t1.astype(bf16)
    r1 = shifted(t1, -2)
    other = swapped(after(state["part", 0, 1], swap1))
    state["dq"] = after(state["dq"], t1)
    stage(state, bwd=[(0, 0)], last=True)
    total = state["part", 0, 0] + other.astype(f32) + r1.astype(f32) + r2.astype(f32)
    return (state["out"], state["grad_q"], total[:, :dim].astype(bf16), total[:, dim:].astype(bf16))


def solution(mesh):
    rows = P(AXES, None)
    return jax.shard_map(
        on_device,
        mesh=mesh,
        in_specs=(rows, rows, rows, rows, P()),
        out_specs=(rows, rows, rows, rows),
        check_vma=False,
    )
```

```python
import functools
import math

import jax
import jax.numpy as jnp
from jax import lax
from jax.experimental import pallas as pl
from jax.experimental.pallas import tpu as pltpu
from jax.sharding import PartitionSpec as P

AXES = ("node", "wide")
MASKED = -1e30
VMEM_LIMIT = 16 * 1024 * 1024
QUICK = pl.CostEstimate(flops=1, bytes_accessed=1, transcendentals=0)
HERE = pl.BlockSpec(memory_space=pltpu.VMEM)


def shifted(shard, by):
    peers = lax.axis_size(AXES)
    pairs = [(i, i + by) for i in range(peers) if 0 <= i + by < peers]
    return lax.ppermute(shard, AXES, pairs)


def swapped(shard):
    peers = lax.axis_size(AXES)
    return lax.ppermute(shard, AXES, [(i, i ^ 1) for i in range(peers)])


def dot_nt(a, b):
    return lax.dot_general(a, b, (((1,), (1,)), ((), ())), preferred_element_type=jnp.float32)


def dot_nn(a, b):
    return lax.dot_general(a, b, (((1,), (0,)), ((), ())), preferred_element_type=jnp.float32)


def beside(keys, values):
    dim = keys.shape[1]
    lane = lax.broadcasted_iota(jnp.int32, (keys.shape[0], 2 * dim), 1)
    none = jnp.zeros((), keys.dtype)
    left = lax.pad(keys, none, ((0, 0, 0), (0, dim, 0)))
    right = lax.pad(values, none, ((0, 0, 0), (dim, 0, 0)))
    return jnp.where(lane < dim, left, right)


def stack_body(q, g, lengths, qs, gs, gt, meta):
    rows, dim = q.shape[0], qs.shape[1]
    docs = lengths.shape[1]
    for h in range(q.shape[1] // dim):
        cols, lanes = slice(h * dim, (h + 1) * dim), slice(h * rows, (h + 1) * rows)
        qs[lanes, :] = q[:, cols]
        gs[lanes, :] = g[:, cols]
        gt[:, lanes] = g[:, cols].T
    device = lax.axis_index(AXES[0]) * lax.axis_size(AXES[1]) + lax.axis_index(AXES[1])
    here = device * rows
    later = lax.broadcasted_iota(jnp.int32, (docs, docs), 0)
    earlier = lax.broadcasted_iota(jnp.int32, (docs, docs), 1)
    counted = jnp.where(earlier <= later, lengths[...].astype(jnp.float32), 0.0)
    ends = jnp.sum(counted, axis=1, keepdims=True)
    pos = (lax.broadcasted_iota(jnp.int32, (docs, rows), 1) + here).astype(jnp.float32)
    start = jnp.max(jnp.where(ends <= pos, ends, 0.0), axis=0, keepdims=True)
    meta[0:1, :] = start.astype(jnp.int32) - here
    meta[1:2, :] = jnp.full((1, rows), device % 2, jnp.int32)


def stack(queries, grad, lengths, dim):
    rows, wide = queries.shape
    tall = jax.ShapeDtypeStruct((rows * wide // dim, dim), queries.dtype)
    return pl.pallas_call(
        stack_body,
        in_specs=[HERE] * 3,
        out_specs=[HERE] * 4,
        out_shape=[
            tall,
            tall,
            jax.ShapeDtypeStruct(tall.shape[::-1], queries.dtype),
            jax.ShapeDtypeStruct((2, rows), jnp.int32),
        ],
        compiler_params=pltpu.CompilerParams(vmem_limit_bytes=VMEM_LIMIT),
    )(queries, grad, lengths)


def stage_body(plan, *refs):
    rows, dim, heads = plan["rows"], plan["dim"], plan["heads"]
    fwd, bwd = plan["fwd"], plan["bwd"]
    ref = dict(zip(plan["names"], refs))
    fold = math.log2(math.e) / math.sqrt(dim)
    scale = 1.0 / math.sqrt(dim)
    bf16, f32 = jnp.bfloat16, jnp.float32
    meta = ref["meta"]
    start = meta[0:1, :]
    earliest = jnp.min(start)
    odd = jnp.max(meta[1:2, :])
    blocks = sorted(set(fwd) | set(bwd))
    cols = [slice(h * dim, (h + 1) * dim) for h in range(heads)]
    lanes = [slice(h * rows, (h + 1) * rows) for h in range(heads)]

    def place(chip, side):
        return (side * (1 - 2 * odd) - 2 * chip) * rows

    def needed(chip, side):
        return (place(chip, side) + rows > earliest) & (place(chip, side) <= 0)

    if plan["first"]:
        ref["m"][...] = jnp.full_like(ref["m"], MASKED)
        ref["l"][...] = jnp.zeros_like(ref["l"])
        ref["acc"][...] = jnp.zeros_like(ref["acc"])

    def load(chip, side):
        block, i = ref["kv", chip, side], blocks.index((chip, side))
        if (chip, side) in fwd:
            ref["vt"][i] = block[:, dim:].T
        if (chip, side) in bwd:
            ref["kt"][i] = block[:, :dim].T

    for block in blocks:
        pl.when(needed(*block))(functools.partial(load, *block))

    def fwd_block(chip, side):
        i = blocks.index((chip, side))
        key_pos = lax.broadcasted_iota(jnp.int32, (rows, rows), 0) + place(chip, side)
        allowed = (key_pos >= start) & (
            key_pos <= lax.broadcasted_iota(jnp.int32, (rows, rows), 1)
        )
        ref["bias"][...] = jnp.where(allowed, 0.0, MASKED)
        block_k, value_t = ref["kv", chip, side][:, :dim], ref["vt"][i]
        for h in range(0, heads, 8):
            wide = slice(h * rows, (h + 8) * rows)
            s = dot_nt(block_k, ref["qs"][wide, :]) + jnp.concatenate([ref["bias"][...]] * 8, axis=1)
            old = ref["m"][:, wide]
            m = jnp.maximum(old, jnp.max(s, axis=0, keepdims=True))
            alpha = jnp.exp2((old - m) * fold)
            p = jnp.exp2((s - m) * fold)
            pb = p.astype(bf16)
            ref["probs", chip, side][:, wide] = pb
            total = jnp.sum(p, axis=0, keepdims=True)
            ref["l"][:, wide] = ref["l"][:, wide] * alpha + total
            ref["acc"][:, wide] = ref["acc"][:, wide] * alpha + dot_nn(value_t, pb)
            ref["m"][:, wide] = m
            ref["then", chip, side][:, wide] = m

    def finish():
        inverse = 1.0 / ref["l"][...]
        o_t = (ref["acc"][...] * inverse).astype(bf16)
        ref["out_t"][...] = o_t
        terms = o_t.astype(f32) * ref["gt"][...].astype(f32)
        ref["delta"][...] = jnp.sum(terms, axis=0, keepdims=True)
        ref["l"][...] = inverse
        ref["dq"][...] = jnp.zeros_like(ref["dq"])

    def bwd_block(chip, side):
        i = blocks.index((chip, side))
        block_v, key_t = ref["kv", chip, side][:, dim:], ref["kt"][i]
        dk = dv = None
        for h in range(0, heads, 8):
            wide = slice(h * rows, (h + 8) * rows)
            dprob = dot_nn(block_v, ref["gt"][:, wide])
            m_then = ref["then", chip, side][:, wide]
            c = jnp.exp2((m_then - ref["m"][:, wide]) * fold) * ref["l"][:, wide]
            p = ref["probs", chip, side][:, wide].astype(f32) * c
            d = (p * (dprob - ref["delta"][:, wide])).astype(bf16)
            p = p.astype(bf16)
            ref["dq"][:, wide] += dot_nn(key_t, d)
            dk_part = dot_nn(d, ref["qs"][wide, :])
            dv_part = dot_nn(p, ref["gs"][wide, :])
            dk = dk_part if dk is None else dk + dk_part
            dv = dv_part if dv is None else dv + dv_part
        part = ref["part", chip, side]
        part[:, :dim] = (dk * scale).astype(part.dtype)
        part[:, dim:] = dv.astype(part.dtype)

    for block in fwd:
        pl.when(needed(*block))(functools.partial(fwd_block, *block))
    if plan["final"]:
        finish()
    for block in bwd:
        part = ref["part", *block]
        pl.when(needed(*block))(functools.partial(bwd_block, *block))

        @pl.when(jnp.logical_not(needed(*block)))
        def _():
            part[...] = jnp.zeros_like(part)

    if plan["last"]:
        for h in range(heads):
            ref["out"][:, cols[h]] = ref["out_t"][:, lanes[h]].T
            ref["grad_q"][:, cols[h]] = (ref["dq"][:, lanes[h]] * scale).astype(bf16).T


def stage(state, fwd=(), bwd=(), final=False, last=False):
    rows, dim2 = state["kv", 0, 0].shape
    dim = dim2 // 2
    width = state["qs"].shape[0]
    heads = width // rows
    bf16, f32 = jnp.bfloat16, jnp.float32
    shape = jax.ShapeDtypeStruct
    blocks = sorted(set(fwd) | set(bwd))
    first = (0, 0) in fwd
    row, tall = shape((1, width), f32), shape((dim, width), f32)
    ins, outs, both = ["meta", "qs"], {}, []
    if final or bwd:
        ins.append("gt")
    if bwd:
        ins.append("gs")
    ins += [("kv", *b) for b in blocks]
    if fwd:
        for b in fwd:
            outs["probs", *b] = shape((rows, width), bf16)
            outs["then", *b] = row
        outs.update(m=row, l=row, acc=tall)
        if not first:
            both += ["m", "l", "acc"]
    if final:
        outs.update(out_t=shape((dim, width), bf16), delta=row, dq=tall)
    if bwd:
        for b in bwd:
            if b not in fwd:
                ins += [("probs", *b), ("then", *b)]
            outs["part", *b] = shape((rows, dim2), bf16 if b[1] else f32)
        if not final:
            ins += ["m", "l", "delta"]
            outs["dq"] = tall
            both.append("dq")
    if last:
        ins.append("out_t")
        outs["out"] = outs["grad_q"] = shape((rows, heads * dim), bf16)
    out_names = list(outs)
    scratch = {}
    if fwd:
        scratch["vt"] = pltpu.VMEM((len(blocks), dim, rows), bf16)
        scratch["bias"] = pltpu.VMEM((rows, rows), f32)
    if bwd:
        scratch["kt"] = pltpu.VMEM((len(blocks), dim, rows), bf16)
    names = ins + [("in", b) for b in both] + out_names + list(scratch)
    plan = dict(
        rows=rows, dim=dim, heads=heads, fwd=fwd, bwd=bwd, first=first, final=final, last=last, names=names
    )
    results = pl.pallas_call(
        functools.partial(stage_body, plan),
        in_specs=[HERE] * (len(ins) + len(both)),
        out_specs=[HERE] * len(out_names),
        out_shape=[outs[n] for n in out_names],
        scratch_shapes=list(scratch.values()),
        input_output_aliases={len(ins) + i: out_names.index(b) for i, b in enumerate(both)},
        compiler_params=pltpu.CompilerParams(vmem_limit_bytes=VMEM_LIMIT),
        cost_estimate=QUICK,
    )(*[state[n] for n in ins + both])
    state.update(zip(out_names, results))


def after(x, *others):
    return lax.optimization_barrier((x, *others))[0]


def pairs(*chips):
    return [(chip, side) for chip in chips for side in (0, 1)]


def on_device(queries, keys, values, out_grad, doc_lengths):
    rows, dim = keys.shape
    f32, bf16 = jnp.float32, jnp.bfloat16
    own = beside(keys, values)
    state = dict(zip(("qs", "gs", "gt", "meta"), stack(queries, out_grad, doc_lengths[None, :], dim)))

    back2 = shifted(own, 4)
    back1 = shifted(after(own, state["qs"]), 2)
    back2 = after(back2, state["qs"])
    back4 = shifted(back2, 4)
    back3 = shifted(back2, 2)
    state["kv", 0, 0], state["kv", 0, 1] = own, swapped(own)
    state["kv", 1, 0] = back1
    state["kv", 2, 0], state["kv", 2, 1] = back2, swapped(back2)
    stage(state, fwd=pairs(0, 2) + [(1, 0)])
    state["kv", 1, 1] = swapped(after(back1, state["l"]))
    for chip, block in ((3, back3), (4, back4)):
        block = after(block, state["l"])
        state["kv", chip, 0], state["kv", chip, 1] = block, swapped(block)
    stage(state, fwd=[(3, 0), (4, 0)])
    stage(state, fwd=[(1, 1), (3, 1), (4, 1)], bwd=[(3, 1), (4, 1)], final=True)
    stage(state, bwd=[(4, 0)])

    def summed(chip, *others):
        other = swapped(after(state["part", chip, 1], *others))
        return state["part", chip, 0] + other.astype(f32), other

    t4, swap4 = summed(4)
    t4 = t4.astype(bf16)
    r4 = shifted(t4, -4)
    state["dq"] = after(state["dq"], t4)
    stage(state, bwd=[(1, 1), (3, 0)])
    t3, swap3 = summed(3, swap4)
    t3 = t3.astype(bf16)
    r3 = shifted(t3, -2)
    state["dq"] = after(state["dq"], t3)
    stage(state, bwd=[(1, 0)])
    t1, _ = summed(1, swap3)
    t1 = t1.astype(bf16)
    r1 = shifted(t1, -2)
    state["dq"] = after(state["dq"], t1)
    stage(state, bwd=pairs(2) + [(0, 1)])
    t2, swap2 = summed(2, r1, r3, r4)
    t2 = (t2 + r4.astype(f32) + r3.astype(f32)).astype(bf16)
    r2 = shifted(t2, -4)
    other = swapped(after(state["part", 0, 1], swap2))
    state["dq"] = after(state["dq"], t2)
    stage(state, bwd=[(0, 0)], last=True)
    total = state["part", 0, 0] + other.astype(f32) + r1.astype(f32) + r2.astype(f32)
    return (state["out"], state["grad_q"], total[:, :dim].astype(bf16), total[:, dim:].astype(bf16))


def solution(mesh):
    rows = P(AXES, None)
    return jax.shard_map(
        on_device,
        mesh=mesh,
        in_specs=(rows, rows, rows, rows, P()),
        out_specs=(rows, rows, rows, rows),
        check_vma=False,
    )
```
